512 devices in a mesh: cols: 128 (over x, z_lo, y), rows: 4 (over z_hi, core).
Axes of the slice: x: 4, y: 8, z: 8 (z_hi: 2, z_lo: 4; z = z_hi * 4 + z_lo), core: 2. Of those that a mesh axis runs over, the one named last changes fastest.
Arguments:
- tokens: bfloat16 [64, 1024, 256], P('rows', 'cols'), may hold values from -600 to 600
- edge_tokens: bfloat16 [2, 3, 1024, 256], P(None, None, 'cols'), may hold values from -18 to 18
- output_grad: bfloat16 [64, 1024, 256], P('rows', 'cols'), may hold values from -24 to 24
- norm_gain: float32 [256], replicated, may hold values from 0.1 to 1.9
- qkv_weight: bfloat16 [256, 768], replicated, may hold values from -0.4 to 0.4
- out_weight: bfloat16 [256, 256], replicated, may hold values from -0.375 to 0.375
- head_scale: float32 [4], replicated, may hold values from 1 to 256
Outputs:
- token_grad: bfloat16 [64, 1024, 256], P('rows', 'cols')
- qkv_grad: float32 [256, 768], P(None, 'cols')
- proj_grad: float32 [256, 256], P(None, 'cols')
- gain_grad: float32 [256], P('cols')
The draws below stay inside these ranges and needn't reach their ends.
All inputs are finite; a program needn't handle non-finite values.
Results may differ from the reference program's by a relative error of at most 0.0087.
Values may be sent and summed in bfloat16 or wider, within the bound.
No kernel may reach another device: no remote copies, remote signals or barrier semaphores. Data moves between devices by JAX's collectives and lax.ppermute only.
A program may use at most 64 MiB of HBM per device.

```python
import math
import jax
import jax.numpy as jnp
from jax import lax

D = 256
HEAD_DIM = 64
HEADS = 4
RADIUS = 3
ROW_DEV = 16
ROWS = 64
WIDTH = 1024
N_ROWS = 4


def draw_tokens(key, part):
    key = jax.random.fold_in(key, 1)
    noise_key, row_key, col_key = jax.random.split(key, 3)
    row_scale = jnp.exp(jax.random.uniform(row_key, (ROWS, WIDTH, 1), jnp.float32) * math.log(10.0))
    col_scale = jnp.exp(jax.random.uniform(col_key, (1, 1, D), jnp.float32, -0.8, 0.8))
    samples = jnp.clip(jax.random.normal(noise_key, (ROWS, WIDTH, D), jnp.float32), -5.0, 5.0)
    return (samples * row_scale * col_scale).astype(jnp.bfloat16)


def draw_qkv_weight(key, part):
    key = jax.random.fold_in(key, 2)
    samples = jnp.clip(jax.random.normal(key, (D, 3 * D), jnp.float32), -5.0, 5.0) * D ** (-0.5)
    return samples.astype(jnp.bfloat16)


def draw_head_scale(key, part):
    key = jax.random.fold_in(key, 3)
    gentle_key = jax.random.fold_in(key, 0)
    return jnp.exp(jax.random.uniform(gentle_key, (HEADS,), jnp.float32, math.log(2.0), math.log(12.0)))


def raised(entries, own_key, source, target, blocks, factor):
    owner, partner = [(jnp.arange(entries.shape[axis_at]) // (entries.shape[axis_at] // blocks)).reshape([-1 if axis == axis_at else 1 for axis in range(entries.ndim)]) for axis_at in (source, target)]
    chosen = jax.random.permutation(own_key, blocks)[partner]
    strong = (owner == chosen) | (owner == (partner + blocks // 2) % blocks)
    return jnp.where(strong, factor * entries, entries)


def level_of(rng, extent, cuts, low, top_value):
    gain, own = 1.0, jax.random.fold_in(rng, 6)
    for dim, shards_of in cuts:
        draws = jnp.exp(jax.random.uniform(jax.random.fold_in(own, dim), (shards_of,), jnp.float32, low / len(cuts), top_value / len(cuts)))
        gain = gain * jnp.repeat(draws, extent[dim] // shards_of).reshape([-1 if axis == dim else 1 for axis in range(len(extent))])
    return gain


def gaussian(key, dims, scale, bound, pieces=(), dtype=jnp.bfloat16):
    result = jax.random.normal(key, dims, jnp.float32) * scale
    if len(pieces) > 0:
        result = level_of(key, dims, pieces, -0.22, 0.18) * result
    return jnp.clip(result, min=-bound, max=bound).astype(dtype)


def heavy_noise(rng, shape, scale, most, pieces, heavy, kind=jnp.bfloat16):
    entries = scale * jax.random.normal(rng, shape, jnp.float32)
    if pieces:
        entries = entries * level_of(rng, shape, pieces, -0.22, 0.18)
    return jnp.clip(raised(entries, jax.random.fold_in(rng, 3), *heavy), -most, most).astype(kind)


def setup_inputs(seed: int = 0) -> dict:
    keys = jax.random.split(jax.random.key(seed), 8)
    tokens = draw_tokens(jax.random.fold_in(keys[7], 71), 0)
    edge_tokens = gaussian(keys[1], (2, RADIUS, WIDTH, D), 3.0, 18.0, ((2, 128),))
    output_grad = heavy_noise(keys[2], (ROWS, WIDTH, D), 1.0, 24.0, ((0, 4), (1, 128)), (1, 2, 128, 5.5))
    norm_gain = jnp.clip(1.0 + 0.18 * jax.random.normal(keys[3], (D,), jnp.float32), 0.1, 1.9)
    qkv_weight = draw_qkv_weight(jax.random.fold_in(keys[7], 71), 0)
    out_weight = gaussian(keys[5], (D, D), D ** -0.5, 0.375)
    head_scale = draw_head_scale(jax.random.fold_in(keys[7], 71), 0)
    return {"tokens": tokens, "edge_tokens": edge_tokens, "output_grad": output_grad, "norm_gain": norm_gain, "qkv_weight": qkv_weight, "out_weight": out_weight, "head_scale": head_scale}


EPSILON = 1e-06
PRECISE = lax.Precision.HIGHEST

def head_norm(raw_values):
    heads_view = raw_values.reshape(raw_values.shape[0], -1, HEAD_DIM)
    reciprocal = lax.rsqrt(lax.optimization_barrier(jnp.mean(heads_view * heads_view, axis=-1, keepdims=True)) + EPSILON)
    return (heads_view * reciprocal, reciprocal)

def head_back(grad_hat, unit_rows, reciprocal):
    return reciprocal * (grad_hat - unit_rows * lax.optimization_barrier(jnp.mean(grad_hat * unit_rows, axis=-1, keepdims=True)))

def project_in(tokens, norm_gain, qkv_weight):
    feature_width = tokens.shape[-1]
    flat_rows = tokens.reshape(-1, feature_width).astype(jnp.float32)
    reciprocal = lax.rsqrt(lax.optimization_barrier(jnp.mean(flat_rows * flat_rows, axis=-1, keepdims=True)) + EPSILON)
    unit_rows = flat_rows * reciprocal
    normed = (unit_rows * norm_gain).astype(jnp.bfloat16)
    projected = jnp.dot(normed, qkv_weight, preferred_element_type=jnp.float32)
    queries, query_recip = head_norm(projected[:, :feature_width])
    key_rows, key_recip = head_norm(projected[:, feature_width:2 * feature_width])
    values = projected[:, 2 * feature_width:]
    return (unit_rows, reciprocal, normed, queries, query_recip, key_rows, key_recip, values)

def key_value(stored, row_count, col_count):
    values = stored[7]
    feature_width = values.shape[1]
    joined = jnp.concatenate([stored[5].reshape(-1, feature_width), values], axis=1)
    return joined.astype(jnp.bfloat16).reshape(row_count, col_count, 2 * feature_width)

def project_back(stored, query_grad, key_grad, value_grad, norm_gain, qkv_weight):
    unit_rows, reciprocal, normed, queries, query_recip, key_rows, key_recip, values = stored
    token_count, feature_width = unit_rows.shape
    raw_query = head_back(query_grad.reshape(queries.shape), queries, query_recip).reshape(token_count, feature_width)
    raw_key = head_back(key_grad.reshape(key_rows.shape), key_rows, key_recip).reshape(token_count, feature_width)
    projected_grad = jnp.concatenate([raw_query, raw_key, value_grad.reshape(token_count, feature_width)], axis=1)
    weight_grad = jnp.dot(normed.astype(jnp.float32).T, projected_grad, precision=PRECISE)
    normed_grad = jnp.dot(projected_grad, qkv_weight.astype(jnp.float32).T, precision=PRECISE)
    gain_part = lax.optimization_barrier(jnp.sum(normed_grad * unit_rows, axis=0))
    scaled = normed_grad * norm_gain
    token_part = reciprocal * (scaled - unit_rows * lax.optimization_barrier(jnp.mean(scaled * unit_rows, axis=-1, keepdims=True)))
    return (token_part, weight_grad, gain_part)

def attend(query_b, padded, upstream, head_scale):
    row_count, col_count, feature_width = query_b.shape
    token_count = row_count * col_count
    head_count = feature_width // HEAD_DIM
    window_span = 2 * RADIUS + 1
    queries = query_b.reshape(token_count, head_count, HEAD_DIM).astype(jnp.float32)
    incoming = upstream.reshape(token_count, head_count, HEAD_DIM).astype(jnp.float32)
    factor = (head_scale / HEAD_DIM)[None, :]
    offsets = [(row_step, col_step) for row_step in range(window_span) for col_step in range(window_span)]

    def window(row_step, col_step):
        block = padded[row_step:row_step + row_count, col_step:col_step + col_count]
        block = block.reshape(token_count, 2, head_count, HEAD_DIM).astype(jnp.float32)
        return (block[:, 0], block[:, 1])
    scores = jnp.stack([lax.optimization_barrier(jnp.sum(queries * window(row_step, col_step)[0], axis=-1)) * factor for row_step, col_step in offsets])
    maximum = lax.optimization_barrier(jnp.max(scores, axis=0))
    exponent = jnp.exp(scores - maximum)
    prob = exponent / lax.optimization_barrier(jnp.sum(exponent, axis=0))
    attended = jnp.zeros((token_count, head_count, HEAD_DIM), jnp.float32)
    products = []
    for position, (row_step, col_step) in enumerate(offsets):
        values = window(row_step, col_step)[1]
        attended = attended + prob[position][:, :, None] * values
        products.append(lax.optimization_barrier(jnp.sum(incoming * values, axis=-1)))
    dot_stack = jnp.stack(products)
    mean_dot = lax.optimization_barrier(jnp.sum(prob * dot_stack, axis=0))
    score_grad = prob * (dot_stack - mean_dot)
    query_grad = jnp.zeros((token_count, head_count, HEAD_DIM), jnp.float32)
    grad_pad = jnp.zeros((row_count + 2 * RADIUS, col_count + 2 * RADIUS, 2 * feature_width), jnp.float32)
    for position, (row_step, col_step) in enumerate(offsets):
        key_rows = window(row_step, col_step)[0]
        weight_rows = (score_grad[position] * factor)[:, :, None]
        query_grad = query_grad + weight_rows * key_rows
        key_grad = (weight_rows * queries).reshape(token_count, feature_width)
        value_grad = (prob[position][:, :, None] * incoming).reshape(token_count, feature_width)
        block = jnp.concatenate([key_grad, value_grad], axis=1).reshape(row_count, col_count, 2 * feature_width)
        grad_pad = grad_pad.at[row_step:row_step + row_count, col_step:col_step + col_count].add(block)
    return (attended.reshape(row_count, col_count, feature_width).astype(jnp.bfloat16), query_grad, grad_pad)

def reference(tokens, edge_tokens, output_grad, norm_gain, qkv_weight, out_weight, head_scale):
    row_total, col_total, feature_width = tokens.shape
    grad_scale = (row_total * col_total) ** (-0.5)
    key_blocks = []
    query_blocks = []
    for block in range(N_ROWS):
        stored = project_in(tokens[block * ROW_DEV:(block + 1) * ROW_DEV], norm_gain, qkv_weight)
        key_blocks.append(key_value(stored, ROW_DEV, col_total))
        query_blocks.append(stored[3].reshape(ROW_DEV, col_total, feature_width).astype(jnp.bfloat16))
    edge_stored = project_in(edge_tokens, norm_gain, qkv_weight)
    edge_kv = key_value(edge_stored, 2 * RADIUS, col_total)
    tall_grid = jnp.concatenate([edge_kv[:RADIUS]] + key_blocks + [edge_kv[RADIUS:]], axis=0)
    wide_grid = jnp.concatenate([tall_grid[:, col_total - RADIUS:], tall_grid, tall_grid[:, :RADIUS]], axis=1)
    grad_total = jnp.zeros((row_total + 2 * RADIUS, col_total + 2 * RADIUS, 2 * feature_width), jnp.float32)
    proj_sum = jnp.zeros((feature_width, feature_width), jnp.float32)
    query_grads = []
    for block in range(N_ROWS):
        lower = block * ROW_DEV
        grad_rows = output_grad[lower:lower + ROW_DEV].reshape(-1, feature_width)
        upstream = jnp.dot(grad_rows, out_weight.T, preferred_element_type=jnp.float32).astype(jnp.bfloat16)
        upstream = upstream.reshape(ROW_DEV, col_total, feature_width)
        attended, query_grad, grad_pad = attend(query_blocks[block], wide_grid[lower:lower + ROW_DEV + 2 * RADIUS], upstream, head_scale)
        grad_total = grad_total.at[lower:lower + ROW_DEV + 2 * RADIUS].add(grad_pad)
        proj_sum = proj_sum + jnp.dot(attended.reshape(-1, feature_width).T, grad_rows, preferred_element_type=jnp.float32)
        query_grads.append(query_grad)
    folded = grad_total[:, RADIUS:col_total + RADIUS]
    folded = folded.at[:, col_total - RADIUS:].add(grad_total[:, :RADIUS])
    folded = folded.at[:, :RADIUS].add(grad_total[:, col_total + RADIUS:])
    qkv_sum = jnp.zeros((feature_width, 3 * feature_width), jnp.float32)
    gain_sum = jnp.zeros((feature_width,), jnp.float32)
    token_rows = []
    for block in range(N_ROWS):
        lower = block * ROW_DEV
        stored = project_in(tokens[lower:lower + ROW_DEV], norm_gain, qkv_weight)
        kv_grad = folded[lower + RADIUS:lower + RADIUS + ROW_DEV].reshape(-1, 2 * feature_width)
        token_part, weight_grad, gain_part = project_back(stored, query_grads[block], kv_grad[:, :feature_width], kv_grad[:, feature_width:], norm_gain, qkv_weight)
        qkv_sum = qkv_sum + weight_grad
        gain_sum = gain_sum + gain_part
        residual = output_grad[lower:lower + ROW_DEV].astype(jnp.float32)
        token_rows.append((residual + token_part.reshape(ROW_DEV, col_total, feature_width)).astype(jnp.bfloat16))
    edge_grad = jnp.concatenate([folded[:RADIUS], folded[RADIUS + row_total:]], axis=0).reshape(-1, 2 * feature_width)
    edge_zero = jnp.zeros((edge_grad.shape[0], feature_width), jnp.float32)
    token_part, weight_grad, gain_part = project_back(edge_stored, edge_zero, edge_grad[:, :feature_width], edge_grad[:, feature_width:], norm_gain, qkv_weight)
    qkv_sum = qkv_sum + weight_grad
    gain_sum = gain_sum + gain_part
    token_grad = jnp.concatenate(token_rows, axis=0)
    return (token_grad, qkv_sum * grad_scale, proj_sum * grad_scale, gain_sum * grad_scale)
```

```python
import jax
import jax.numpy as jnp
from jax import lax
from jax.experimental import pallas as pl
from jax.experimental.pallas import tpu as pltpu
from jax.sharding import PartitionSpec as P

HEAD_DIM = 64
HEADS = 4
RADIUS = 3
EPSILON = 1e-06

SPAN = 32
REACH = 2 * RADIUS
BAND = 4
LOWEST = -1e30
F32 = jnp.float32
BF16 = jnp.bfloat16


def dot(left, right, left_dim=1, right_dim=0):
    return lax.dot_general(
        left, right, (((left_dim,), (right_dim,)), ((), ())), preferred_element_type=F32
    )


def head_mean(values, group):
    high = values.astype(BF16)
    low = (values - high.astype(F32)).astype(BF16)
    return (dot(high, group) + dot(low, group)) * (1.0 / HEAD_DIM)


def unit_norm(cells):
    rows = cells.astype(F32)
    reciprocal = lax.rsqrt(jnp.mean(rows * rows, axis=-1, keepdims=True) + EPSILON)
    return rows * reciprocal, reciprocal


def head_norm(raw, group):
    reciprocal = lax.rsqrt(head_mean(raw * raw, group) + EPSILON)
    return raw * reciprocal, reciprocal


def head_back(grad, hat, reciprocal, group):
    return reciprocal * (grad - hat * head_mean(grad * hat, group))


def block_kernel(
    place_ref, scale_ref, own_ref, own_grad_ref, west_ref, east_ref, gain_ref, qkv_ref, out_ref,
    token_ref, qkv_grad_ref, proj_grad_ref, gain_grad_ref,
    key_ref, value_ref, key_grad_ref, value_grad_ref,
):
    width = own_ref.shape[1]
    own_count = own_ref.shape[0]
    strip = REACH * SPAN
    top = place_ref[0] == 0
    bottom = place_ref[0] == place_ref[1] - 1
    gain = gain_ref[...]
    weight = qkv_ref[...]
    lane_head = lax.broadcasted_iota(jnp.int32, (width, width), 0) // HEAD_DIM
    group = (lane_head == lax.broadcasted_iota(jnp.int32, (width, width), 1) // HEAD_DIM).astype(BF16)

    def row_in(count):
        return lax.broadcasted_iota(jnp.int32, (count, 1), 0) & (SPAN - 1)

    def query_rows(count):
        row = row_in(count)
        own = row < 16
        below = (row >= 16) & (row < 16 + RADIUS) & jnp.logical_not(bottom)
        above = (row >= SPAN - RADIUS) & jnp.logical_not(top)
        return own | below | above

    def keys_of(cells, start):
        unit, reciprocal = unit_norm(cells)
        normed = (unit * gain).astype(BF16)
        keys, key_recip = head_norm(dot(normed, weight[:, width : 2 * width]), group)
        values = dot(normed, weight[:, 2 * width :])
        key_ref[start : start + cells.shape[0]] = keys.astype(BF16)
        value_ref[start : start + cells.shape[0]] = values.astype(BF16)
        return unit, reciprocal, normed, keys, key_recip

    def queries_of(normed):
        return head_norm(dot(normed, weight[:, :width]), group)

    unit, reciprocal, normed, keys, key_recip = keys_of(own_ref[...], strip)
    queries, query_recip = queries_of(normed)
    west_normed = keys_of(west_ref[:strip], 0)[2]
    east_normed = keys_of(east_ref[:strip], strip + own_count)[2]
    band = BAND * SPAN
    west_query = queries_of(west_normed[strip - band :])[0]
    east_query = queries_of(east_normed[:band])[0]

    own_grad = own_grad_ref[...]
    out_weight = out_ref[...]
    own_up = dot(own_grad, out_weight, 1, 1)
    west_up = dot(west_ref[strip:], out_weight, 1, 1)
    east_up = dot(east_ref[strip:], out_weight, 1, 1)
    empty = jnp.zeros((SPAN, width), F32)

    lane = lax.broadcasted_iota(jnp.int32, (1, width), 1) // HEAD_DIM
    zero = jnp.zeros((), BF16)

    def spread(cells, valid):
        cells = jnp.where(valid, cells, 0.0).astype(BF16)
        return jnp.concatenate([jnp.where(lane == head, cells, zero) for head in range(HEADS)], axis=0)

    rows_ok = query_rows(band)
    strip_col = lax.broadcasted_iota(jnp.int32, (band, 1), 0) // SPAN
    bands = (
        (spread(west_query, rows_ok & (strip_col > 0)), jnp.concatenate([empty, west_up], axis=0)),
        (spread(queries[:band], rows_ok), own_up[:band]),
        (spread(queries[band:], rows_ok), own_up[band:]),
        (spread(east_query, rows_ok & (strip_col < RADIUS)), jnp.concatenate([east_up, empty], axis=0)),
    )

    deep = (BAND + REACH) * SPAN
    key_at = lax.broadcasted_iota(jnp.int32, (deep, band), 0)
    query_at = lax.broadcasted_iota(jnp.int32, (deep, band), 1)
    col_gap = key_at // SPAN - query_at // SPAN
    row_gap = (key_at - query_at + RADIUS) & (SPAN - 1)
    inside = (col_gap >= 0) & (col_gap <= REACH) & (row_gap <= REACH)
    bias = jnp.where(inside, 0.0, LOWEST)
    bias = jnp.concatenate([bias] * HEADS, axis=1)
    factor = jnp.concatenate(
        [jnp.full((1, band), scale_ref[head] * (1.0 / HEAD_DIM), F32) for head in range(HEADS)], axis=1
    )

    def merge(stacked):
        half = width // 2
        low = lax.broadcasted_iota(jnp.int32, (1, half), 1) < HEAD_DIM
        parts = [stacked[head * band : (head + 1) * band] for head in range(HEADS)]
        return jnp.concatenate(
            [
                jnp.where(low, parts[0][:, :half], parts[1][:, :half]),
                jnp.where(low, parts[2][:, half:], parts[3][:, half:]),
            ],
            axis=1,
        )

    key_grad_ref[...] = jnp.zeros_like(key_grad_ref)
    value_grad_ref[...] = jnp.zeros_like(value_grad_ref)
    attended = []
    query_grads = []
    own_end = strip + own_count
    for index, (query_big, upstream) in enumerate(bands):
        up_big = spread(upstream, rows_ok)
        first = (2 + BAND * index - RADIUS) * SPAN
        last = first + deep
        lower, upper = max(first, 0), min(last, own_end + strip)
        key_band = key_ref[lower:upper]
        value_band = value_ref[lower:upper]
        scores = dot(key_band, query_big, 1, 1) * factor + bias[lower - first : upper - first]
        exponent = jnp.exp(scores - jnp.max(scores, axis=0, keepdims=True))
        prob = exponent * (1.0 / jnp.sum(exponent, axis=0, keepdims=True))
        dots = dot(value_band, up_big, 1, 1)
        mean_dot = jnp.sum(prob * dots, axis=0, keepdims=True)
        weighted = (prob * (dots - mean_dot) * factor).astype(BF16)
        prob = prob.astype(BF16)
        near, far = max(lower, strip), min(upper, own_end)
        key_grad_ref[near - strip : far - strip] += dot(weighted[near - lower : far - lower], query_big)
        value_grad_ref[near - strip : far - strip] += dot(prob[near - lower : far - lower], up_big)
        if index in (1, 2):
            attended.append(merge(dot(prob, value_band, 0, 0)))
            query_grads.append(merge(dot(weighted, key_band, 0, 0)))

    row = row_in(own_count)
    own_rows = row < 16
    key_rows = own_rows | (top & (row >= SPAN - RADIUS)) | (bottom & (row >= 16) & (row < 16 + RADIUS))
    query_grad = jnp.concatenate(query_grads, axis=0)
    raw_query = head_back(query_grad, queries, query_recip, group)
    raw_key = head_back(key_grad_ref[...], keys, key_recip, group)
    projected_grad = jnp.concatenate(
        [
            jnp.where(own_rows, raw_query, 0.0),
            jnp.where(key_rows, raw_key, 0.0),
            jnp.where(key_rows, value_grad_ref[...], 0.0),
        ],
        axis=1,
    ).astype(BF16)
    normed_grad = dot(projected_grad, weight, 1, 1)
    gain_grad_ref[...] = jnp.sum(normed_grad * unit, axis=0, keepdims=True)
    scaled = normed_grad * gain
    token_part = reciprocal * (scaled - unit * jnp.mean(scaled * unit, axis=-1, keepdims=True))
    token_ref[...] = (own_grad.astype(F32) + token_part).astype(BF16)
    qkv_grad_ref[...] = dot(projected_grad, normed, 0, 0).astype(BF16)
    attended = jnp.where(own_rows, jnp.concatenate(attended, axis=0), 0.0).astype(BF16)
    proj_grad_ref[...] = dot(own_grad, attended, 0, 0).astype(BF16)


def exchange(axis, count, closed, to_next, to_back):
    ends = count if closed else count - 1
    from_back = lax.ppermute(to_next, axis, [(i, (i + 1) % count) for i in range(ends)])
    from_next = lax.ppermute(to_back, axis, [((i + 1) % count, i) for i in range(ends)])
    return from_back, from_next


def on_device(tokens, edge_tokens, output_grad, norm_gain, qkv_weight, out_weight, head_scale):
    row_count, col_count, width = tokens.shape
    row_devices = lax.axis_size("rows")
    col_devices = lax.axis_size("cols")
    place = lax.axis_index("rows")
    grad_scale = (row_count * row_devices * col_count * col_devices) ** (-0.5)
    own = tokens.transpose(1, 0, 2)
    grad = output_grad.transpose(1, 0, 2)
    edges = edge_tokens.transpose(2, 0, 1, 3)
    above, below = exchange(
        "rows",
        row_devices,
        False,
        jnp.concatenate([own[:, row_count - REACH :], grad[:, row_count - RADIUS :]], axis=1),
        jnp.concatenate([own[:, :REACH], grad[:, :RADIUS]], axis=1),
    )
    blank = jnp.zeros((col_count, RADIUS, width), BF16)
    upper = jnp.where(place == 0, jnp.concatenate([blank, edges[:, 0]], axis=1), above[:, :REACH])
    lower = jnp.where(
        place == row_devices - 1, jnp.concatenate([edges[:, 1], blank], axis=1), below[:, :REACH]
    )
    gap = jnp.zeros((col_count, SPAN - row_count - 2 * REACH, width), BF16)
    slab = jnp.concatenate([own, lower, gap, upper], axis=1)
    grad_gap = jnp.zeros((col_count, SPAN - row_count - 2 * RADIUS, width), BF16)
    grad_slab = jnp.concatenate([grad, below[:, REACH:], grad_gap, above[:, REACH:]], axis=1)
    west, east = exchange(
        "cols",
        col_devices,
        True,
        jnp.concatenate([slab[col_count - REACH :], grad_slab[col_count - RADIUS :]], axis=0),
        jnp.concatenate([slab[:REACH], grad_slab[:RADIUS]], axis=0),
    )
    cells = col_count * SPAN
    whole = pl.BlockSpec(memory_space=pltpu.VMEM)
    scalars = pl.BlockSpec(memory_space=pltpu.SMEM)
    token_grad, qkv_grad, proj_grad, gain_grad = pl.pallas_call(
        block_kernel,
        out_shape=(
            jax.ShapeDtypeStruct((cells, width), BF16),
            jax.ShapeDtypeStruct((3 * width, width), BF16),
            jax.ShapeDtypeStruct((width, width), BF16),
            jax.ShapeDtypeStruct((1, width), F32),
        ),
        in_specs=[scalars, scalars] + [whole] * 7,
        out_specs=(whole,) * 4,
        scratch_shapes=[
            pltpu.VMEM((cells + 2 * REACH * SPAN, width), BF16),
            pltpu.VMEM((cells + 2 * REACH * SPAN, width), BF16),
            pltpu.VMEM((cells, width), F32),
            pltpu.VMEM((cells, width), F32),
        ],
        compiler_params=pltpu.CompilerParams(vmem_limit_bytes=40 * 2**20),
    )(
        jnp.stack([place, row_devices]).astype(jnp.int32),
        head_scale,
        slab.reshape(cells, width),
        grad_slab.reshape(cells, width),
        west.reshape(-1, width),
        east.reshape(-1, width),
        norm_gain[None, :],
        qkv_weight,
        out_weight,
    )
    token_grad = token_grad.reshape(col_count, SPAN, width)[:, :row_count].transpose(1, 0, 2)
    share = width // col_devices
    chunks = jnp.concatenate(
        [
            qkv_grad.reshape(col_devices, 3 * share, width),
            proj_grad.reshape(col_devices, share, width),
        ],
        axis=1,
    )
    gains = jnp.pad(
        gain_grad.astype(BF16).reshape(col_devices, 1, share),
        ((0, 0), (0, 4 * share - 1), (0, 128 - share)),
    )
    chunks = jnp.concatenate([chunks, gains], axis=2)
    chunks = lax.all_to_all(chunks, "cols", 0, 0)
    part = jnp.sum(chunks.astype(F32), axis=0)
    part = jnp.sum(lax.all_gather(part, "rows", axis=0), axis=0) * grad_scale
    return (
        token_grad,
        part[: 3 * share, :width].T,
        part[3 * share :, :width].T,
        part[0, width : width + share],
    )


def solution(mesh):
    return jax.shard_map(
        on_device,
        mesh=mesh,
        in_specs=(
            P("rows", "cols", None),
            P(None, None, "cols", None),
            P("rows", "cols", None),
            P(),
            P(),
            P(),
            P(),
        ),
        out_specs=(P("rows", "cols", None), P(None, "cols"), P(None, "cols"), P("cols")),
        check_vma=False,
    )
```

```python
import jax
import jax.numpy as jnp
import ml_dtypes
import numpy as np
from jax import lax
from jax.experimental import pallas as pl
from jax.experimental.pallas import tpu as pltpu
from jax.sharding import PartitionSpec as P

HEAD_DIM = 64
HEADS = 4
RADIUS = 3
EPSILON = 1e-06

SPAN = 32
REACH = 2 * RADIUS
BAND = 4
LANES = 128
LOWEST = -1e30
F32 = jnp.float32
BF16 = jnp.bfloat16


def dot(left, right, left_dim=1, right_dim=0):
    return lax.dot_general(
        left, right, (((left_dim,), (right_dim,)), ((), ())), preferred_element_type=F32
    )


def head_mean(values, group):
    high = values.astype(BF16)
    low = (values - high.astype(F32)).astype(BF16)
    return (dot(high, group) + dot(low, group)) * (1.0 / HEAD_DIM)


def unit_norm(cells):
    rows = cells.astype(F32)
    reciprocal = lax.rsqrt(jnp.mean(rows * rows, axis=-1, keepdims=True) + EPSILON)
    return rows * reciprocal, reciprocal


def head_norm(raw, group):
    reciprocal = lax.rsqrt(head_mean(raw * raw, group) + EPSILON)
    return raw * reciprocal, reciprocal


def head_back(grad, hat, reciprocal, group):
    return reciprocal * (grad - hat * head_mean(grad * hat, group))


def block_kernel(
    place_ref, scale_ref, own_ref, own_grad_ref, west_ref, east_ref, gain_ref, qkv_ref, out_ref, pick_ref,
    token_ref, keep_ref, send_ref,
    key_ref, value_ref, key_grad_ref, value_grad_ref,
):
    width = own_ref.shape[1]
    own_count = own_ref.shape[0]
    strip = REACH * SPAN
    top = place_ref[0] == 0
    bottom = place_ref[0] == place_ref[1] - 1
    gain = gain_ref[...]
    weight = qkv_ref[...]
    lane_head = lax.broadcasted_iota(jnp.int32, (width, width), 0) // HEAD_DIM
    group = (lane_head == lax.broadcasted_iota(jnp.int32, (width, width), 1) // HEAD_DIM).astype(BF16)

    def row_in(count):
        return lax.broadcasted_iota(jnp.int32, (count, 1), 0) & (SPAN - 1)

    def query_rows(count):
        row = row_in(count)
        own = row < 16
        below = (row >= 16) & (row < 16 + RADIUS) & jnp.logical_not(bottom)
        above = (row >= SPAN - RADIUS) & jnp.logical_not(top)
        return own | below | above

    def keys_of(cells, start):
        unit, reciprocal = unit_norm(cells)
        normed = (unit * gain).astype(BF16)
        keys, key_recip = head_norm(dot(normed, weight[:, width : 2 * width]), group)
        values = dot(normed, weight[:, 2 * width :])
        key_ref[start : start + cells.shape[0]] = keys.astype(BF16)
        value_ref[start : start + cells.shape[0]] = values.astype(BF16)
        return unit, reciprocal, normed, keys, key_recip

    def queries_of(normed):
        return head_norm(dot(normed, weight[:, :width]), group)

    unit, reciprocal, normed, keys, key_recip = keys_of(own_ref[...], strip)
    queries, query_recip = queries_of(normed)
    west_normed = keys_of(west_ref[:strip], 0)[2]
    east_normed = keys_of(east_ref[:strip], strip + own_count)[2]
    band = BAND * SPAN
    west_query = queries_of(west_normed[strip - band :])[0]
    east_query = queries_of(east_normed[:band])[0]

    own_grad = own_grad_ref[...]
    out_weight = out_ref[...]
    own_up = dot(own_grad, out_weight, 1, 1)
    west_up = dot(west_ref[strip:], out_weight, 1, 1)
    east_up = dot(east_ref[strip:], out_weight, 1, 1)
    empty = jnp.zeros((SPAN, width), F32)

    lane = lax.broadcasted_iota(jnp.int32, (1, width), 1) // HEAD_DIM
    zero = jnp.zeros((), BF16)

    def spread(cells, valid):
        cells = jnp.where(valid, cells, 0.0).astype(BF16)
        return jnp.concatenate([jnp.where(lane == head, cells, zero) for head in range(HEADS)], axis=0)

    rows_ok = query_rows(band)
    strip_col = lax.broadcasted_iota(jnp.int32, (band, 1), 0) // SPAN
    bands = (
        (spread(west_query, rows_ok & (strip_col > 0)), jnp.concatenate([empty, west_up], axis=0)),
        (spread(queries[:band], rows_ok), own_up[:band]),
        (spread(queries[band:], rows_ok), own_up[band:]),
        (spread(east_query, rows_ok & (strip_col < RADIUS)), jnp.concatenate([east_up, empty], axis=0)),
    )

    deep = (BAND + REACH) * SPAN
    key_at = lax.broadcasted_iota(jnp.int32, (deep, band), 0)
    query_at = lax.broadcasted_iota(jnp.int32, (deep, band), 1)
    col_gap = key_at // SPAN - query_at // SPAN
    row_gap = (key_at - query_at + RADIUS) & (SPAN - 1)
    inside = (col_gap >= 0) & (col_gap <= REACH) & (row_gap <= REACH)
    bias = jnp.where(inside, 0.0, LOWEST)
    bias = jnp.concatenate([bias] * HEADS, axis=1)
    factor = jnp.concatenate(
        [jnp.full((1, band), scale_ref[head] * (1.0 / HEAD_DIM), F32) for head in range(HEADS)], axis=1
    )

    def merge(stacked):
        half = width // 2
        low = lax.broadcasted_iota(jnp.int32, (1, half), 1) < HEAD_DIM
        parts = [stacked[head * band : (head + 1) * band] for head in range(HEADS)]
        return jnp.concatenate(
            [
                jnp.where(low, parts[0][:, :half], parts[1][:, :half]),
                jnp.where(low, parts[2][:, half:], parts[3][:, half:]),
            ],
            axis=1,
        )

    key_grad_ref[...] = jnp.zeros_like(key_grad_ref)
    value_grad_ref[...] = jnp.zeros_like(value_grad_ref)
    attended = []
    query_grads = []
    own_end = strip + own_count
    for index, (query_big, upstream) in enumerate(bands):
        up_big = spread(upstream, rows_ok)
        first = (2 + BAND * index - RADIUS) * SPAN
        last = first + deep
        lower, upper = max(first, 0), min(last, own_end + strip)
        key_band = key_ref[lower:upper]
        value_band = value_ref[lower:upper]
        scores = dot(key_band, query_big, 1, 1) * factor + bias[lower - first : upper - first]
        exponent = jnp.exp(scores - jnp.max(scores, axis=0, keepdims=True))
        prob = exponent * (1.0 / jnp.sum(exponent, axis=0, keepdims=True))
        dots = dot(value_band, up_big, 1, 1)
        mean_dot = jnp.sum(prob * dots, axis=0, keepdims=True)
        weighted = (prob * (dots - mean_dot) * factor).astype(BF16)
        prob = prob.astype(BF16)
        near, far = max(lower, strip), min(upper, own_end)
        key_grad_ref[near - strip : far - strip] += dot(weighted[near - lower : far - lower], query_big)
        value_grad_ref[near - strip : far - strip] += dot(prob[near - lower : far - lower], up_big)
        if index in (1, 2):
            attended.append(merge(dot(prob, value_band, 0, 0)))
            query_grads.append(merge(dot(weighted, key_band, 0, 0)))

    row = row_in(own_count)
    own_rows = row < 16
    key_rows = own_rows | (top & (row >= SPAN - RADIUS)) | (bottom & (row >= 16) & (row < 16 + RADIUS))
    query_grad = jnp.concatenate(query_grads, axis=0)
    raw_query = head_back(query_grad, queries, query_recip, group)
    raw_key = head_back(key_grad_ref[...], keys, key_recip, group)
    projected_grad = jnp.concatenate(
        [
            jnp.where(own_rows, raw_query, 0.0),
            jnp.where(key_rows, raw_key, 0.0),
            jnp.where(key_rows, value_grad_ref[...], 0.0),
        ],
        axis=1,
    ).astype(BF16)
    normed_grad = dot(projected_grad, weight, 1, 1)
    gain_grad = jnp.sum(normed_grad * unit, axis=0, keepdims=True)
    scaled = normed_grad * gain
    token_part = reciprocal * (scaled - unit * jnp.mean(scaled * unit, axis=-1, keepdims=True))
    token_ref[...] = (own_grad.astype(F32) + token_part).astype(BF16)
    attended = jnp.where(own_rows, jnp.concatenate(attended, axis=0), 0.0).astype(BF16)
    factors = jnp.concatenate([normed, attended], axis=0)
    gain_rows = jnp.broadcast_to(gain_grad, (LANES, width)).astype(BF16)
    for half, half_ref in enumerate((keep_ref, send_ref)):
        pick = pick_ref[(place_ref[0] + half) % 2]
        columns = jnp.concatenate(
            [
                dot(projected_grad, pick[: 3 * width]).astype(BF16),
                dot(own_grad, pick[3 * width : 4 * width]).astype(BF16),
            ],
            axis=0,
        )
        half_ref[:, :width] = dot(columns, factors, 0, 0).astype(BF16)
        half_ref[:, width:] = dot(pick[4 * width :], gain_rows, 0, 1).astype(BF16)


def picks(width, col_devices):
    share = width // col_devices
    part = share // 2
    rows = 4 * part
    half, source, target = np.ogrid[:2, : 5 * width, : col_devices * rows]
    chunk, row = target // rows, target % rows
    weight = chunk * 3 * share + half * 3 * part + row
    output = 3 * width + chunk * share + half * part + row - 3 * part
    gain = 4 * width + chunk * share + half * part + row
    chosen = (source == np.where(row < 3 * part, weight, output)) | ((source == gain) & (row < part))
    return chosen.astype(ml_dtypes.bfloat16)


def exchange(axis, count, closed, to_next, to_back):
    ends = count if closed else count - 1
    from_back = lax.ppermute(to_next, axis, [(i, (i + 1) % count) for i in range(ends)])
    from_next = lax.ppermute(to_back, axis, [((i + 1) % count, i) for i in range(ends)])
    return from_back, from_next


def on_device(tokens, edge_tokens, output_grad, norm_gain, qkv_weight, out_weight, head_scale):
    row_count, col_count, width = tokens.shape
    row_devices = lax.axis_size("rows")
    col_devices = lax.axis_size("cols")
    place = lax.axis_index("rows")
    grad_scale = (row_count * row_devices * col_count * col_devices) ** (-0.5)
    own = tokens.transpose(1, 0, 2)
    grad = output_grad.transpose(1, 0, 2)
    edges = edge_tokens.transpose(2, 0, 1, 3)
    above, below = exchange(
        "rows",
        row_devices,
        False,
        jnp.concatenate([own[:, row_count - REACH :], grad[:, row_count - RADIUS :]], axis=1),
        jnp.concatenate([own[:, :REACH], grad[:, :RADIUS]], axis=1),
    )
    blank = jnp.zeros((col_count, RADIUS, width), BF16)
    upper = jnp.where(place == 0, jnp.concatenate([blank, edges[:, 0]], axis=1), above[:, :REACH])
    lower = jnp.where(
        place == row_devices - 1, jnp.concatenate([edges[:, 1], blank], axis=1), below[:, :REACH]
    )
    gap = jnp.zeros((col_count, SPAN - row_count - 2 * REACH, width), BF16)
    slab = jnp.concatenate([own, lower, gap, upper], axis=1)
    grad_gap = jnp.zeros((col_count, SPAN - row_count - 2 * RADIUS, width), BF16)
    grad_slab = jnp.concatenate([grad, below[:, REACH:], grad_gap, above[:, REACH:]], axis=1)
    west, east = exchange(
        "cols",
        col_devices,
        True,
        jnp.concatenate([slab[col_count - REACH :], grad_slab[col_count - RADIUS :]], axis=0),
        jnp.concatenate([slab[:REACH], grad_slab[:RADIUS]], axis=0),
    )
    cells = col_count * SPAN
    whole = pl.BlockSpec(memory_space=pltpu.VMEM)
    scalars = pl.BlockSpec(memory_space=pltpu.SMEM)
    token_grad, keep, send = pl.pallas_call(
        block_kernel,
        out_shape=(
            jax.ShapeDtypeStruct((cells, width), BF16),
            jax.ShapeDtypeStruct((2 * width, width + LANES), BF16),
            jax.ShapeDtypeStruct((2 * width, width + LANES), BF16),
        ),
        in_specs=[scalars, scalars] + [whole] * 8,
        out_specs=(whole,) * 3,
        scratch_shapes=[
            pltpu.VMEM((cells + 2 * REACH * SPAN, width), BF16),
            pltpu.VMEM((cells + 2 * REACH * SPAN, width), BF16),
            pltpu.VMEM((cells, width), F32),
            pltpu.VMEM((cells, width), F32),
        ],
        compiler_params=pltpu.CompilerParams(vmem_limit_bytes=40 * 2**20),
    )(
        jnp.stack([place, row_devices]).astype(jnp.int32),
        head_scale,
        slab.reshape(cells, width),
        grad_slab.reshape(cells, width),
        west.reshape(-1, width),
        east.reshape(-1, width),
        norm_gain[None, :],
        qkv_weight,
        out_weight,
        picks(width, col_devices),
    )
    token_grad = token_grad.reshape(col_count, SPAN, width)[:, :row_count].transpose(1, 0, 2)
    received = lax.ppermute(send, "rows", [(i, i ^ 1) for i in range(row_devices)])
    chunks = (keep.astype(F32) + received.astype(F32)).astype(BF16)
    share = width // col_devices
    part = share // 2
    chunks = lax.all_to_all(chunks.reshape(col_devices, 4 * part, width + LANES), "cols", 0, 0)
    blocks = jnp.sum(chunks.astype(F32), axis=0).reshape(4 * part, -1, LANES).transpose(1, 0, 2)
    blocks = jnp.pad(blocks.reshape(-1, LANES), ((0, 4 * part), (0, 0)))
    blocks = lax.all_gather(blocks, "rows", axis=0, tiled=True)
    blocks = blocks.reshape(2, 2, -1, 4 * part, LANES)[:, :, :-1]
    halves = (blocks[0] + blocks[1]).transpose(0, 2, 1, 3).reshape(2, 4 * part, -1) * grad_scale
    return (
        token_grad,
        halves[:, : 3 * part, :width].reshape(3 * share, width).T,
        halves[:, 3 * part :, :width].reshape(share, width).T,
        halves[:, :part, width].reshape(share),
    )


def solution(mesh):
    return jax.shard_map(
        on_device,
        mesh=mesh,
        in_specs=(
            P("rows", "cols", None),
            P(None, None, "cols", None),
            P("rows", "cols", None),
            P(),
            P(),
            P(),
            P(),
        ),
        out_specs=(P("rows", "cols", None), P(None, "cols"), P(None, "cols"), P("cols")),
        check_vma=False,
    )
```

```python
import functools

import jax
import jax.numpy as jnp
from jax import lax
from jax.experimental import pallas as pl
from jax.experimental.pallas import tpu as pltpu
from jax.sharding import PartitionSpec as P

HEAD_DIM = 64
HEADS = 4
RADIUS = 3
EPSILON = 1e-06

SPAN = 32
REACH = 2 * RADIUS
BAND = 4
LANES = 128
LOWEST = -1e30
F32 = jnp.float32
BF16 = jnp.bfloat16


def dot(left, right, left_dim=1, right_dim=0):
    return lax.dot_general(
        left, right, (((left_dim,), (right_dim,)), ((), ())), preferred_element_type=F32
    )


def head_mean(values, group):
    high = values.astype(BF16)
    low = (values - high.astype(F32)).astype(BF16)
    return (dot(high, group) + dot(low, group)) * (1.0 / HEAD_DIM)


def unit_norm(cells):
    rows = cells.astype(F32)
    reciprocal = lax.rsqrt(jnp.mean(rows * rows, axis=-1, keepdims=True) + EPSILON)
    return rows * reciprocal, reciprocal


def head_norm(raw, group):
    reciprocal = lax.rsqrt(head_mean(raw * raw, group) + EPSILON)
    return raw * reciprocal, reciprocal


def head_back(grad, hat, reciprocal, group):
    return reciprocal * (grad - hat * head_mean(grad * hat, group))


def block_kernel(
    place_ref, scale_ref, own_ref, own_grad_ref, odd_ref, even_ref, gain_ref, qkv_ref, out_ref,
    token_ref, chunk_ref,
    key_ref, value_ref, key_grad_ref, value_grad_ref, weight_grad_ref,
):
    width = own_ref.shape[1]
    own_count = own_ref.shape[0]
    strip = REACH * SPAN
    top = place_ref[0] == 0
    bottom = place_ref[0] == place_ref[1] - 1
    parity = place_ref[2]
    odd_strip, even_strip = odd_ref[...], even_ref[1 - parity]
    west = jnp.where(parity == 0, odd_strip, even_strip)
    east = jnp.where(parity == 0, even_strip, odd_strip)
    gain = gain_ref[...]
    weight = qkv_ref[...]
    lane_head = lax.broadcasted_iota(jnp.int32, (width, width), 0) // HEAD_DIM
    group = (lane_head == lax.broadcasted_iota(jnp.int32, (width, width), 1) // HEAD_DIM).astype(BF16)

    def row_in(count):
        return lax.broadcasted_iota(jnp.int32, (count, 1), 0) & (SPAN - 1)

    def query_rows(count):
        row = row_in(count)
        own = row < 16
        below = (row >= 16) & (row < 16 + RADIUS) & jnp.logical_not(bottom)
        above = (row >= SPAN - RADIUS) & jnp.logical_not(top)
        return own | below | above

    def keys_of(cells, start):
        unit, reciprocal = unit_norm(cells)
        normed = (unit * gain).astype(BF16)
        keys, key_recip = head_norm(dot(normed, weight[:, width : 2 * width]), group)
        values = dot(normed, weight[:, 2 * width :])
        key_ref[start : start + cells.shape[0]] = keys.astype(BF16)
        value_ref[start : start + cells.shape[0]] = values.astype(BF16)
        return unit, reciprocal, normed, keys, key_recip

    def queries_of(normed):
        return head_norm(dot(normed, weight[:, :width]), group)

    unit, reciprocal, normed, keys, key_recip = keys_of(own_ref[...], strip)
    queries, query_recip = queries_of(normed)
    west_normed = keys_of(west[:strip], 0)[2]
    east_normed = keys_of(east[:strip], strip + own_count)[2]
    band = BAND * SPAN
    west_query = queries_of(west_normed[strip - band :])[0]
    east_query = queries_of(east_normed[:band])[0]

    own_grad = own_grad_ref[...]
    out_weight = out_ref[...]
    own_up = dot(own_grad, out_weight, 1, 1)
    west_up = dot(west[strip:], out_weight, 1, 1)
    east_up = dot(east[strip:], out_weight, 1, 1)
    empty = jnp.zeros((SPAN, width), F32)

    lane = lax.broadcasted_iota(jnp.int32, (1, width), 1) // HEAD_DIM
    zero = jnp.zeros((), BF16)

    def spread(cells, valid):
        cells = jnp.where(valid, cells, 0.0).astype(BF16)
        return jnp.concatenate([jnp.where(lane == head, cells, zero) for head in range(HEADS)], axis=0)

    rows_ok = query_rows(band)
    strip_col = lax.broadcasted_iota(jnp.int32, (band, 1), 0) // SPAN
    bands = (
        (spread(west_query, rows_ok & (strip_col > 0)), jnp.concatenate([empty, west_up], axis=0)),
        (spread(queries[:band], rows_ok), own_up[:band]),
        (spread(queries[band:], rows_ok), own_up[band:]),
        (spread(east_query, rows_ok & (strip_col < RADIUS)), jnp.concatenate([east_up, empty], axis=0)),
    )

    deep = (BAND + REACH) * SPAN
    key_at = lax.broadcasted_iota(jnp.int32, (deep, band), 0)
    query_at = lax.broadcasted_iota(jnp.int32, (deep, band), 1)
    col_gap = key_at // SPAN - query_at // SPAN
    row_gap = (key_at - query_at + RADIUS) & (SPAN - 1)
    inside = (col_gap >= 0) & (col_gap <= REACH) & (row_gap <= REACH)
    bias = jnp.where(inside, 0.0, LOWEST)
    bias = jnp.concatenate([bias] * HEADS, axis=1)
    factor = jnp.concatenate(
        [jnp.full((1, band), scale_ref[head] * (1.0 / HEAD_DIM), F32) for head in range(HEADS)], axis=1
    )

    def merge(stacked):
        half = width // 2
        low = lax.broadcasted_iota(jnp.int32, (1, half), 1) < HEAD_DIM
        parts = [stacked[head * band : (head + 1) * band] for head in range(HEADS)]
        return jnp.concatenate(
            [
                jnp.where(low, parts[0][:, :half], parts[1][:, :half]),
                jnp.where(low, parts[2][:, half:], parts[3][:, half:]),
            ],
            axis=1,
        )

    key_grad_ref[...] = jnp.zeros_like(key_grad_ref)
    value_grad_ref[...] = jnp.zeros_like(value_grad_ref)
    attended = []
    query_grads = []
    own_end = strip + own_count
    for index, (query_big, upstream) in enumerate(bands):
        up_big = spread(upstream, rows_ok)
        first = (2 + BAND * index - RADIUS) * SPAN
        last = first + deep
        lower, upper = max(first, 0), min(last, own_end + strip)
        key_band = key_ref[lower:upper]
        value_band = value_ref[lower:upper]
        scores = dot(key_band, query_big, 1, 1) * factor + bias[lower - first : upper - first]
        exponent = jnp.exp(scores - jnp.max(scores, axis=0, keepdims=True))
        prob = exponent * (1.0 / jnp.sum(exponent, axis=0, keepdims=True))
        dots = dot(value_band, up_big, 1, 1)
        mean_dot = jnp.sum(prob * dots, axis=0, keepdims=True)
        weighted = (prob * (dots - mean_dot) * factor).astype(BF16)
        prob = prob.astype(BF16)
        near, far = max(lower, strip), min(upper, own_end)
        key_grad_ref[near - strip : far - strip] += dot(weighted[near - lower : far - lower], query_big)
        value_grad_ref[near - strip : far - strip] += dot(prob[near - lower : far - lower], up_big)
        if index in (1, 2):
            attended.append(merge(dot(prob, value_band, 0, 0)))
            query_grads.append(merge(dot(weighted, key_band, 0, 0)))

    row = row_in(own_count)
    own_rows = row < 16
    key_rows = own_rows | (top & (row >= SPAN - RADIUS)) | (bottom & (row >= 16) & (row < 16 + RADIUS))
    query_grad = jnp.concatenate(query_grads, axis=0)
    raw_query = head_back(query_grad, queries, query_recip, group)
    raw_key = head_back(key_grad_ref[...], keys, key_recip, group)
    projected_grad = jnp.concatenate(
        [
            jnp.where(own_rows, raw_query, 0.0),
            jnp.where(key_rows, raw_key, 0.0),
            jnp.where(key_rows, value_grad_ref[...], 0.0),
        ],
        axis=1,
    ).astype(BF16)
    normed_grad = dot(projected_grad, weight, 1, 1)
    gain_grad = jnp.sum(normed_grad * unit, axis=0, keepdims=True)
    scaled = normed_grad * gain
    token_part = reciprocal * (scaled - unit * jnp.mean(scaled * unit, axis=-1, keepdims=True))
    token_ref[...] = (own_grad.astype(F32) + token_part).astype(BF16)
    weight_grad = dot(projected_grad, normed, 0, 0)
    blocks = range(width // LANES)
    for block in blocks:
        weight_grad_ref[block] = weight_grad[:, block * LANES : (block + 1) * LANES]
    attended = jnp.where(own_rows, jnp.concatenate(attended, axis=0), 0.0).astype(BF16)
    for part in range(3):
        for block in blocks:
            third = weight_grad_ref.at[block][pl.ds(part, width, stride=3), :]
            at = part * width + block * LANES
            chunk_ref[:, at : at + LANES] = third.astype(BF16)
    chunk_ref[:, 3 * width : 4 * width] = dot(own_grad, attended, 0, 0).astype(BF16)
    chunk_ref[:, 4 * width :] = jnp.broadcast_to(gain_grad, (LANES, width)).T.astype(BF16)


def final_kernel(scale, parts_ref, qkv_ref, proj_ref, gain_ref):
    share, width = proj_ref.shape
    rows = parts_ref.shape[0] // 4
    total = sum(parts_ref[part * rows : (part + 1) * rows] for part in range(4)) * scale
    lane = lax.broadcasted_iota(jnp.int32, (1, LANES), 1)
    gain = jnp.zeros((1, LANES), F32)
    step = 4 * (width // LANES) + 1
    for side in range(share):
        at = side * step
        for part in range(4):
            row = jnp.concatenate([total[at : at + 1], total[at + 1 : at + 2]], axis=1)
            if part < 3:
                qkv_ref[3 * side + part : 3 * side + part + 1, :] = row
            else:
                proj_ref[side : side + 1, :] = row
            at += 2
        gain = jnp.where(lane == side, total[at : at + 1], gain)
    gain_ref[...] = gain[:, :share]


def on_device(tokens, edge_tokens, output_grad, norm_gain, qkv_weight, out_weight, head_scale):
    row_count, col_count, width = tokens.shape
    row_devices = lax.axis_size("rows")
    col_devices = lax.axis_size("cols")
    place = lax.axis_index("rows")
    grad_scale = (row_count * row_devices * col_count * col_devices) ** (-0.5)
    parity = lax.axis_index("cols") & 1
    strips = jnp.concatenate(
        [
            tokens[:REACH],
            tokens[row_count - REACH :],
            output_grad[:RADIUS],
            output_grad[row_count - RADIUS :],
        ],
        axis=0,
    )
    strips = lax.all_gather(strips, "rows", axis=0).transpose(0, 2, 1, 3)
    above = strips[jnp.maximum(place - 1, 0)]
    below = strips[jnp.minimum(place + 1, row_devices - 1)]
    own = tokens.transpose(1, 0, 2)
    grad = output_grad.transpose(1, 0, 2)
    edges = edge_tokens.transpose(2, 0, 1, 3)
    blank = jnp.zeros((col_count, RADIUS, width), BF16)
    upper = jnp.where(
        place == 0, jnp.concatenate([blank, edges[:, 0]], axis=1), above[:, REACH : 2 * REACH]
    )
    lower = jnp.where(
        place == row_devices - 1, jnp.concatenate([edges[:, 1], blank], axis=1), below[:, :REACH]
    )
    gap = jnp.zeros((col_count, SPAN - row_count - 2 * REACH, width), BF16)
    slab = jnp.concatenate([own, lower, gap, upper], axis=1)
    grad_gap = jnp.zeros((col_count, SPAN - row_count - 2 * RADIUS, width), BF16)
    grad_slab = jnp.concatenate(
        [
            grad,
            below[:, 2 * REACH : 2 * REACH + RADIUS],
            grad_gap,
            above[:, 2 * REACH + RADIUS :],
        ],
        axis=1,
    )
    facing_west = jnp.concatenate([slab[:REACH], grad_slab[:RADIUS]], axis=0)
    facing_east = jnp.concatenate([slab[col_count - REACH :], grad_slab[col_count - RADIUS :]], axis=0)
    first = [i for i in range(1, col_devices, 2)]
    pairs = [(i, (i + 1) % col_devices) for i in first]
    odd = lax.ppermute(
        jnp.where(parity == 0, facing_west, facing_east), "cols", pairs + [(b, a) for a, b in pairs]
    )
    even = lax.all_gather(
        jnp.where(parity == 0, facing_east, facing_west),
        "cols",
        axis=0,
        axis_index_groups=[[i, i + 1] for i in range(0, col_devices, 2)],
    )
    cells = col_count * SPAN
    whole = pl.BlockSpec(memory_space=pltpu.VMEM)
    scalars = pl.BlockSpec(memory_space=pltpu.SMEM)
    token_grad, chunks = pl.pallas_call(
        block_kernel,
        out_shape=(
            jax.ShapeDtypeStruct((cells, width), BF16),
            jax.ShapeDtypeStruct((width, 4 * width + LANES), BF16),
        ),
        in_specs=[scalars, scalars] + [whole] * 7,
        out_specs=(whole,) * 2,
        scratch_shapes=[
            pltpu.VMEM((cells + 2 * REACH * SPAN, width), BF16),
            pltpu.VMEM((cells + 2 * REACH * SPAN, width), BF16),
            pltpu.VMEM((cells, width), F32),
            pltpu.VMEM((cells, width), F32),
            pltpu.VMEM((width // LANES, 3 * width, LANES), F32),
        ],
        compiler_params=pltpu.CompilerParams(vmem_limit_bytes=40 * 2**20),
    )(
        jnp.stack([place, row_devices, parity]).astype(jnp.int32),
        head_scale,
        slab.reshape(cells, width),
        grad_slab.reshape(cells, width),
        odd.reshape(-1, width),
        even.reshape(2, -1, width),
        norm_gain[None, :],
        qkv_weight,
        out_weight,
    )
    token_grad = token_grad.reshape(col_count, SPAN, width)[:, :row_count].transpose(1, 0, 2)
    share = width // col_devices
    chunks = lax.all_to_all(chunks.reshape(col_devices, share, -1), "cols", 0, 0)
    part = jnp.sum(chunks.astype(F32), axis=0).reshape(-1, LANES)
    part = jnp.pad(part, ((0, -part.shape[0] % 8), (0, 0)))
    qkv_grad, proj_grad, gain_grad = pl.pallas_call(
        functools.partial(final_kernel, grad_scale),
        out_shape=(
            jax.ShapeDtypeStruct((3 * share, width), F32),
            jax.ShapeDtypeStruct((share, width), F32),
            jax.ShapeDtypeStruct((1, share), F32),
        ),
        in_specs=[whole],
        out_specs=(whole,) * 3,
    )(lax.all_gather(part, "rows", axis=0, tiled=True))
    return token_grad, qkv_grad.T, proj_grad.T, gain_grad.reshape(share)


def solution(mesh):
    return jax.shard_map(
        on_device,
        mesh=mesh,
        in_specs=(
            P("rows", "cols", None),
            P(None, None, "cols", None),
            P("rows", "cols", None),
            P(),
            P(),
            P(),
            P(),
        ),
        out_specs=(P("rows", "cols", None), P(None, "cols"), P(None, "cols"), P("cols")),
        check_vma=False,
    )
```

```python
import functools

import jax
import jax.numpy as jnp
from jax import lax
from jax.experimental import pallas as pl
from jax.experimental.pallas import tpu as pltpu
from jax.sharding import PartitionSpec as P

HEAD_DIM = 64
HEADS = 4
RADIUS = 3
EPSILON = 1e-06

SPAN = 32
REACH = 2 * RADIUS
BAND = 4
LANES = 128
TAIL = 16
COLS = ("x", "l", "y")
ROWS = ("h", "c")
SPLIT = (4, 4, 8)
LOWEST = -1e30
F32 = jnp.float32
BF16 = jnp.bfloat16


def dot(left, right, left_dim=1, right_dim=0):
    return lax.dot_general(
        left, right, (((left_dim,), (right_dim,)), ((), ())), preferred_element_type=F32
    )


def head_mean(values, group):
    high = values.astype(BF16)
    low = (values - high.astype(F32)).astype(BF16)
    return (dot(high, group) + dot(low, group)) * (1.0 / HEAD_DIM)


def unit_norm(cells):
    rows = cells.astype(F32)
    reciprocal = lax.rsqrt(jnp.mean(rows * rows, axis=-1, keepdims=True) + EPSILON)
    return rows * reciprocal, reciprocal


def head_norm(raw, group):
    reciprocal = lax.rsqrt(head_mean(raw * raw, group) + EPSILON)
    return raw * reciprocal, reciprocal


def head_back(grad, hat, reciprocal, group):
    return reciprocal * (grad - hat * head_mean(grad * hat, group))


def block_kernel(
    place_ref, scale_ref, own_ref, own_grad_ref, odd_ref, even_ref, gain_ref, qkv_ref, out_ref,
    token_ref, chunk_ref,
    key_ref, value_ref, key_grad_ref, value_grad_ref, weight_grad_ref, proj_grad_ref,
):
    width = own_ref.shape[1]
    own_count = own_ref.shape[0]
    strip = REACH * SPAN
    top = place_ref[0] == 0
    bottom = place_ref[0] == place_ref[1] - 1
    parity = place_ref[2]
    odd_strip, even_strip = odd_ref[...], even_ref[1 - parity]
    west = jnp.where(parity == 0, odd_strip, even_strip)
    east = jnp.where(parity == 0, even_strip, odd_strip)
    gain = gain_ref[...]
    weight = qkv_ref[...]
    lane_head = lax.broadcasted_iota(jnp.int32, (width, width), 0) // HEAD_DIM
    group = (lane_head == lax.broadcasted_iota(jnp.int32, (width, width), 1) // HEAD_DIM).astype(BF16)

    def row_in(count):
        return lax.broadcasted_iota(jnp.int32, (count, 1), 0) & (SPAN - 1)

    def query_rows(count):
        row = row_in(count)
        own = row < 16
        below = (row >= 16) & (row < 16 + RADIUS) & jnp.logical_not(bottom)
        above = (row >= SPAN - RADIUS) & jnp.logical_not(top)
        return own | below | above

    def keys_of(cells, start):
        unit, reciprocal = unit_norm(cells)
        normed = (unit * gain).astype(BF16)
        keys, key_recip = head_norm(dot(normed, weight[:, width : 2 * width]), group)
        values = dot(normed, weight[:, 2 * width :])
        key_ref[start : start + cells.shape[0]] = keys.astype(BF16)
        value_ref[start : start + cells.shape[0]] = values.astype(BF16)
        return unit, reciprocal, normed, keys, key_recip

    def queries_of(normed):
        return head_norm(dot(normed, weight[:, :width]), group)

    unit, reciprocal, normed, keys, key_recip = keys_of(own_ref[...], strip)
    queries, query_recip = queries_of(normed)
    west_normed = keys_of(west[:strip], 0)[2]
    east_normed = keys_of(east[:strip], strip + own_count)[2]
    band = BAND * SPAN
    west_query = queries_of(west_normed[strip - band :])[0]
    east_query = queries_of(east_normed[:band])[0]

    own_grad = own_grad_ref[...]
    out_weight = out_ref[...]
    own_up = dot(own_grad, out_weight, 1, 1)
    west_up = dot(west[strip:], out_weight, 1, 1)
    east_up = dot(east[strip:], out_weight, 1, 1)
    empty = jnp.zeros((SPAN, width), F32)

    lane = lax.broadcasted_iota(jnp.int32, (1, width), 1) // HEAD_DIM
    zero = jnp.zeros((), BF16)

    def spread(cells, valid):
        cells = jnp.where(valid, cells, 0.0).astype(BF16)
        return jnp.concatenate([jnp.where(lane == head, cells, zero) for head in range(HEADS)], axis=0)

    rows_ok = query_rows(band)
    strip_col = lax.broadcasted_iota(jnp.int32, (band, 1), 0) // SPAN
    bands = (
        (spread(west_query, rows_ok & (strip_col > 0)), jnp.concatenate([empty, west_up], axis=0)),
        (spread(queries[:band], rows_ok), own_up[:band]),
        (spread(queries[band:], rows_ok), own_up[band:]),
        (spread(east_query, rows_ok & (strip_col < RADIUS)), jnp.concatenate([east_up, empty], axis=0)),
    )

    deep = (BAND + REACH) * SPAN
    key_at = lax.broadcasted_iota(jnp.int32, (deep, band), 0)
    query_at = lax.broadcasted_iota(jnp.int32, (deep, band), 1)
    col_gap = key_at // SPAN - query_at // SPAN
    row_gap = (key_at - query_at + RADIUS) & (SPAN - 1)
    inside = (col_gap >= 0) & (col_gap <= REACH) & (row_gap <= REACH)
    bias = jnp.where(inside, 0.0, LOWEST)
    bias = jnp.concatenate([bias] * HEADS, axis=1)
    factor = jnp.concatenate(
        [jnp.full((1, band), scale_ref[head] * (1.0 / HEAD_DIM), F32) for head in range(HEADS)], axis=1
    )

    def merge(stacked):
        half = width // 2
        low = lax.broadcasted_iota(jnp.int32, (1, half), 1) < HEAD_DIM
        parts = [stacked[head * band : (head + 1) * band] for head in range(HEADS)]
        return jnp.concatenate(
            [
                jnp.where(low, parts[0][:, :half], parts[1][:, :half]),
                jnp.where(low, parts[2][:, half:], parts[3][:, half:]),
            ],
            axis=1,
        )

    key_grad_ref[...] = jnp.zeros_like(key_grad_ref)
    value_grad_ref[...] = jnp.zeros_like(value_grad_ref)
    attended = []
    query_grads = []
    own_end = strip + own_count
    for index, (query_big, upstream) in enumerate(bands):
        up_big = spread(upstream, rows_ok)
        first = (2 + BAND * index - RADIUS) * SPAN
        last = first + deep
        lower, upper = max(first, 0), min(last, own_end + strip)
        key_band = key_ref[lower:upper]
        value_band = value_ref[lower:upper]
        scores = dot(key_band, query_big, 1, 1) * factor + bias[lower - first : upper - first]
        exponent = jnp.exp(scores - jnp.max(scores, axis=0, keepdims=True))
        prob = exponent * (1.0 / jnp.sum(exponent, axis=0, keepdims=True))
        dots = dot(value_band, up_big, 1, 1)
        mean_dot = jnp.sum(prob * dots, axis=0, keepdims=True)
        weighted = (prob * (dots - mean_dot) * factor).astype(BF16)
        prob = prob.astype(BF16)
        near, far = max(lower, strip), min(upper, own_end)
        key_grad_ref[near - strip : far - strip] += dot(weighted[near - lower : far - lower], query_big)
        value_grad_ref[near - strip : far - strip] += dot(prob[near - lower : far - lower], up_big)
        if index in (1, 2):
            attended.append(merge(dot(prob, value_band, 0, 0)))
            query_grads.append(merge(dot(weighted, key_band, 0, 0)))

    row = row_in(own_count)
    own_rows = row < 16
    key_rows = own_rows | (top & (row >= SPAN - RADIUS)) | (bottom & (row >= 16) & (row < 16 + RADIUS))
    query_grad = jnp.concatenate(query_grads, axis=0)
    raw_query = head_back(query_grad, queries, query_recip, group)
    raw_key = head_back(key_grad_ref[...], keys, key_recip, group)
    projected_grad = jnp.concatenate(
        [
            jnp.where(own_rows, raw_query, 0.0),
            jnp.where(key_rows, raw_key, 0.0),
            jnp.where(key_rows, value_grad_ref[...], 0.0),
        ],
        axis=1,
    ).astype(BF16)
    normed_grad = dot(projected_grad, weight, 1, 1)
    gain_grad = jnp.sum(normed_grad * unit, axis=0, keepdims=True)
    scaled = normed_grad * gain
    token_part = reciprocal * (scaled - unit * jnp.mean(scaled * unit, axis=-1, keepdims=True))
    token_ref[...] = (own_grad.astype(F32) + token_part).astype(BF16)
    attended = jnp.where(own_rows, jnp.concatenate(attended, axis=0), 0.0).astype(BF16)
    weight_grad = dot(projected_grad, normed, 0, 0)
    proj_grad = dot(own_grad, attended, 0, 0)
    for block in range(width // LANES):
        at = slice(block * LANES, (block + 1) * LANES)
        weight_grad_ref[block] = weight_grad[:, at]
        proj_grad_ref[block] = proj_grad[:, at]
    blocks, rows = chunk_ref.shape[:2]
    group = (rows - TAIL) // 8
    for peer in range(blocks):
        line, side = peer // 2, peer % 2
        for part in range(4):
            for block in range(width // LANES):
                if part < 3:
                    start = 6 * group * line + 3 * side + part
                    cells = weight_grad_ref.at[block][pl.ds(start, group, stride=6), :]
                else:
                    start = 2 * group * line + side
                    cells = proj_grad_ref.at[block][pl.ds(start, group, stride=2), :]
                at = (2 * part + block) * group
                chunk_ref[peer, at : at + group] = cells.astype(BF16)
        lanes = gain_grad[:, 2 * group * line // LANES * LANES :][:, :LANES]
        chunk_ref[peer, rows - TAIL :] = jnp.broadcast_to(lanes, (TAIL, LANES)).astype(BF16)


def middle_kernel(chunk_ref, part_ref, sum_ref):
    group = sum_ref.shape[0] // 8
    copies = part_ref.shape[0] // group
    total = sum(chunk_ref[peer].astype(F32) for peer in range(chunk_ref.shape[0]))
    sum_ref[...] = total[: 8 * group]
    gains = total[8 * group : 8 * group + TAIL - 8]
    for column in range(group):
        rows = jnp.concatenate([sum_ref[pl.ds(column, 8, stride=group), :], gains], axis=0).astype(BF16)
        for copy in range(copies):
            part_ref[copies * column + copy] = rows


def final_kernel(scale, place_ref, parts_ref, qkv_ref, proj_ref, gain_ref):
    total = parts_ref[...] * scale
    lane = lax.broadcasted_iota(jnp.int32, (1, LANES), 1)
    gains = []
    for side in range(2):
        for part in range(4):
            at = side * TAIL + 2 * part
            row = jnp.concatenate([total[at : at + 1], total[at + 1 : at + 2]], axis=1)
            if part < 3:
                qkv_ref[3 * side + part : 3 * side + part + 1, :] = row
            else:
                proj_ref[side : side + 1, :] = row
        here = lane == 2 * place_ref[0] % LANES + side
        gains.append(jnp.sum(jnp.where(here, total[at + 2 : at + 3], 0.0), axis=1, keepdims=True))
    gain_ref[...] = jnp.concatenate(gains, axis=1)


def on_device(tokens, edge_tokens, output_grad, norm_gain, qkv_weight, out_weight, head_scale):
    row_count, col_count, width = tokens.shape
    row_devices = lax.axis_size(ROWS)
    col_devices = lax.axis_size(COLS)
    place = lax.axis_index(ROWS)
    grad_scale = (row_count * row_devices * col_count * col_devices) ** (-0.5)
    parity = lax.axis_index(COLS) & 1
    strips = jnp.concatenate(
        [
            tokens[:REACH],
            tokens[row_count - REACH :],
            output_grad[:RADIUS],
            output_grad[row_count - RADIUS :],
        ],
        axis=0,
    )
    strips = lax.all_gather(strips, ROWS, axis=0).transpose(0, 2, 1, 3)
    above = strips[jnp.maximum(place - 1, 0)]
    below = strips[jnp.minimum(place + 1, row_devices - 1)]
    own = tokens.transpose(1, 0, 2)
    grad = output_grad.transpose(1, 0, 2)
    edges = edge_tokens.transpose(2, 0, 1, 3)
    blank = jnp.zeros((col_count, RADIUS, width), BF16)
    upper = jnp.where(
        place == 0, jnp.concatenate([blank, edges[:, 0]], axis=1), above[:, REACH : 2 * REACH]
    )
    lower = jnp.where(
        place == row_devices - 1, jnp.concatenate([edges[:, 1], blank], axis=1), below[:, :REACH]
    )
    gap = jnp.zeros((col_count, SPAN - row_count - 2 * REACH, width), BF16)
    slab = jnp.concatenate([own, lower, gap, upper], axis=1)
    grad_gap = jnp.zeros((col_count, SPAN - row_count - 2 * RADIUS, width), BF16)
    grad_slab = jnp.concatenate(
        [
            grad,
            below[:, 2 * REACH : 2 * REACH + RADIUS],
            grad_gap,
            above[:, 2 * REACH + RADIUS :],
        ],
        axis=1,
    )
    facing_west = jnp.concatenate([slab[:REACH], grad_slab[:RADIUS]], axis=0)
    facing_east = jnp.concatenate([slab[col_count - REACH :], grad_slab[col_count - RADIUS :]], axis=0)
    first = [i for i in range(1, col_devices, 2)]
    pairs = [(i, (i + 1) % col_devices) for i in first]
    odd = lax.ppermute(
        jnp.where(parity == 0, facing_west, facing_east), COLS, pairs + [(b, a) for a, b in pairs]
    )
    even = lax.all_gather(
        jnp.where(parity == 0, facing_east, facing_west),
        COLS,
        axis=0,
        axis_index_groups=[[i, i + 1] for i in range(0, col_devices, 2)],
    )
    cells = col_count * SPAN
    lines = lax.axis_size("x")
    group = col_devices // lines
    whole = pl.BlockSpec(memory_space=pltpu.VMEM)
    scalars = pl.BlockSpec(memory_space=pltpu.SMEM)
    token_grad, chunks = pl.pallas_call(
        block_kernel,
        out_shape=(
            jax.ShapeDtypeStruct((cells, width), BF16),
            jax.ShapeDtypeStruct((2 * lines, 8 * group + TAIL, LANES), BF16),
        ),
        in_specs=[scalars, scalars] + [whole] * 7,
        out_specs=(whole,) * 2,
        scratch_shapes=[
            pltpu.VMEM((cells + 2 * REACH * SPAN, width), BF16),
            pltpu.VMEM((cells + 2 * REACH * SPAN, width), BF16),
            pltpu.VMEM((cells, width), F32),
            pltpu.VMEM((cells, width), F32),
            pltpu.VMEM((width // LANES, 3 * width, LANES), F32),
            pltpu.VMEM((width // LANES, width, LANES), F32),
        ],
        compiler_params=pltpu.CompilerParams(vmem_limit_bytes=40 * 2**20),
    )(
        jnp.stack([place, row_devices, parity]).astype(jnp.int32),
        head_scale,
        slab.reshape(cells, width),
        grad_slab.reshape(cells, width),
        odd.reshape(-1, width),
        even.reshape(2, -1, width),
        norm_gain[None, :],
        qkv_weight,
        out_weight,
    )
    token_grad = token_grad.reshape(col_count, SPAN, width)[:, :row_count].transpose(1, 0, 2)
    chunks = lax.all_to_all(chunks, ("x", "c"), 0, 0)
    halves = lax.axis_size("h")
    part = pl.pallas_call(
        middle_kernel,
        out_shape=jax.ShapeDtypeStruct((halves * group, TAIL, LANES), BF16),
        in_specs=[whole],
        out_specs=whole,
        scratch_shapes=[pltpu.VMEM((8 * group, LANES), F32)],
    )(chunks)
    part = jnp.sum(lax.all_to_all(part, ("l", "y", "h"), 0, 0).astype(F32), axis=0)
    qkv_grad, proj_grad, gain_grad = pl.pallas_call(
        functools.partial(final_kernel, grad_scale),
        out_shape=(
            jax.ShapeDtypeStruct((6, width), F32),
            jax.ShapeDtypeStruct((2, width), F32),
            jax.ShapeDtypeStruct((1, 2), F32),
        ),
        in_specs=[scalars, whole],
        out_specs=(whole,) * 3,
    )(lax.axis_index(COLS)[None].astype(jnp.int32), lax.all_gather(part, "c", axis=0, tiled=True))
    return token_grad, qkv_grad.T, proj_grad.T, gain_grad.reshape(2)


def solution(mesh):
    parts = SPLIT + (2, 2)
    fine = jax.sharding.Mesh(mesh.devices.reshape(parts), COLS + ROWS)
    return jax.shard_map(
        on_device,
        mesh=fine,
        in_specs=(
            P(ROWS, COLS, None),
            P(None, None, COLS, None),
            P(ROWS, COLS, None),
            P(),
            P(),
            P(),
            P(),
        ),
        out_specs=(P(ROWS, COLS, None), P(None, COLS), P(None, COLS), P(COLS)),
        check_vma=False,
    )
```

```python
import functools
import math

import jax
import jax.numpy as jnp
from jax import lax
from jax.experimental import pallas as pl
from jax.experimental.pallas import tpu as pltpu
from jax.sharding import PartitionSpec as P

HEAD_DIM = 64
HEADS = 4
RADIUS = 3
EPSILON = 1e-06

SPAN = 32
REACH = 2 * RADIUS
BAND = 4
LANES = 128
TAIL = 16
COLS = ("x", "l", "y")
ROWS = ("h", "c")
SPLIT = (4, 4, 8)
LOWEST = -1e30
F32 = jnp.float32
BF16 = jnp.bfloat16


def dot(left, right, left_dim=1, right_dim=0):
    return lax.dot_general(
        left, right, (((left_dim,), (right_dim,)), ((), ())), preferred_element_type=F32
    )


def head_mean(values, group):
    high = values.astype(BF16)
    low = (values - high.astype(F32)).astype(BF16)
    return (dot(high, group) + dot(low, group)) * (1.0 / HEAD_DIM)


def unit_norm(cells):
    rows = cells.astype(F32)
    reciprocal = lax.rsqrt(jnp.mean(rows * rows, axis=-1, keepdims=True) + EPSILON)
    return rows * reciprocal, reciprocal


def head_norm(raw, group):
    reciprocal = lax.rsqrt(head_mean(raw * raw, group) + EPSILON)
    return raw * reciprocal, reciprocal


def head_back(grad, hat, reciprocal, group):
    return reciprocal * (grad - hat * head_mean(grad * hat, group))


def head_group(width):
    head = lax.broadcasted_iota(jnp.int32, (width, width), 0) // HEAD_DIM
    return (head == lax.broadcasted_iota(jnp.int32, (width, width), 1) // HEAD_DIM).astype(BF16)


def own_kernel(
    head_ref, own_ref, own_grad_ref, gain_ref, qkv_ref, out_ref,
    factor_ref, unit_ref, scale_ref, normed_ref, key_ref, key_recip_ref, key_b_ref, value_b_ref, query_ref, query_recip_ref, up_ref,
):
    width = own_ref.shape[1]
    lane = lax.broadcasted_iota(jnp.int32, (1, width), 1) // HEAD_DIM
    factor_ref[...] = jnp.zeros_like(factor_ref)
    for head in range(HEADS):
        factor = jnp.broadcast_to(head_ref[:, head : head + 1] * (1.0 / HEAD_DIM), (1, width))
        factor_ref[:1] = jnp.where(lane == head, factor, factor_ref[:1])
    weight = qkv_ref[...]
    group = head_group(width)
    unit, reciprocal = unit_norm(own_ref[...])
    normed = (unit * gain_ref[...]).astype(BF16)
    keys, key_recip = head_norm(dot(normed, weight[:, width : 2 * width]), group)
    queries, query_recip = head_norm(dot(normed, weight[:, :width]), group)
    unit_ref[...] = unit
    scale_ref[...] = jnp.broadcast_to(reciprocal, scale_ref.shape)
    normed_ref[...] = normed
    key_ref[...] = keys
    key_recip_ref[...] = key_recip
    key_b_ref[...] = keys.astype(BF16)
    value_b_ref[...] = dot(normed, weight[:, 2 * width :]).astype(BF16)
    query_ref[...] = queries
    query_recip_ref[...] = query_recip
    up_ref[...] = dot(own_grad_ref[...], out_ref[...], 1, 1)


def block_kernel(
    place_ref, own_grad_ref, odd_ref, even_ref, gain_ref, qkv_ref, out_ref,
    factor_ref, own_unit_ref, own_scale_ref, own_normed_ref, own_key_ref, own_key_recip_ref, own_key_b_ref, own_value_b_ref,
    own_query_ref, own_query_recip_ref, own_up_ref,
    token_ref, chunk_ref,
    key_ref, value_ref, key_grad_ref, value_grad_ref, weight_grad_ref, proj_grad_ref,
):
    own_count, width = own_grad_ref.shape
    strip = REACH * SPAN
    top = place_ref[0] == 0
    bottom = place_ref[0] == place_ref[1] - 1
    parity = place_ref[2]
    odd_strip, even_strip = odd_ref[...], even_ref[1 - parity]
    west = jnp.where(parity == 0, odd_strip, even_strip)
    east = jnp.where(parity == 0, even_strip, odd_strip)
    gain = gain_ref[...]
    weight = qkv_ref[...]
    group = head_group(width)

    def row_in(count):
        return lax.broadcasted_iota(jnp.int32, (count, 1), 0) & (SPAN - 1)

    def query_rows(count):
        row = row_in(count)
        own = row < 16
        below = (row >= 16) & (row < 16 + RADIUS) & jnp.logical_not(bottom)
        above = (row >= SPAN - RADIUS) & jnp.logical_not(top)
        return own | below | above

    def keys_of(cells, start):
        unit, reciprocal = unit_norm(cells)
        normed = (unit * gain).astype(BF16)
        keys, key_recip = head_norm(dot(normed, weight[:, width : 2 * width]), group)
        values = dot(normed, weight[:, 2 * width :])
        key_ref[start : start + cells.shape[0]] = keys.astype(BF16)
        value_ref[start : start + cells.shape[0]] = values.astype(BF16)
        return normed

    def queries_of(normed):
        return head_norm(dot(normed, weight[:, :width]), group)

    key_ref[strip : strip + own_count] = own_key_b_ref[...]
    value_ref[strip : strip + own_count] = own_value_b_ref[...]
    queries = own_query_ref[...]
    west_normed = keys_of(west[:strip], 0)
    east_normed = keys_of(east[:strip], strip + own_count)
    band = BAND * SPAN
    west_query = queries_of(west_normed[strip - band :])[0]
    east_query = queries_of(east_normed[:band])[0]

    own_grad = own_grad_ref[...]
    out_weight = out_ref[...]
    own_up = own_up_ref[...]
    west_up = dot(west[strip:], out_weight, 1, 1)
    east_up = dot(east[strip:], out_weight, 1, 1)
    empty = jnp.zeros((SPAN, width), F32)

    lane = lax.broadcasted_iota(jnp.int32, (1, width), 1) // HEAD_DIM
    zero = jnp.zeros((), BF16)

    def spread(cells, valid):
        cells = jnp.where(valid, cells, 0.0).astype(BF16)
        return jnp.concatenate([jnp.where(lane == head, cells, zero) for head in range(HEADS)], axis=0)

    rows_ok = query_rows(band)
    strip_col = lax.broadcasted_iota(jnp.int32, (band, 1), 0) // SPAN
    bands = (
        (spread(west_query, rows_ok & (strip_col > 0)), jnp.concatenate([empty, west_up], axis=0)),
        (spread(queries[:band], rows_ok), own_up[:band]),
        (spread(queries[band:], rows_ok), own_up[band:]),
        (spread(east_query, rows_ok & (strip_col < RADIUS)), jnp.concatenate([east_up, empty], axis=0)),
    )

    deep = (BAND + REACH) * SPAN
    key_at = lax.broadcasted_iota(jnp.int32, (deep, band), 0)
    query_at = lax.broadcasted_iota(jnp.int32, (deep, band), 1)
    col_gap = key_at // SPAN - query_at // SPAN
    row_gap = (key_at - query_at + RADIUS) & (SPAN - 1)
    inside = (col_gap >= 0) & (col_gap <= REACH) & (row_gap <= REACH)
    bias = jnp.where(inside, 0.0, LOWEST)
    bias = jnp.concatenate([bias] * HEADS, axis=1)
    head_factor = factor_ref[:1]
    factor = jnp.concatenate(
        [
            jnp.broadcast_to(head_factor[:, head * HEAD_DIM : head * HEAD_DIM + 1], (1, band))
            for head in range(HEADS)
        ],
        axis=1,
    ) * math.log2(math.e)

    def merge(stacked):
        half = width // 2
        low = lax.broadcasted_iota(jnp.int32, (1, half), 1) < HEAD_DIM
        parts = [stacked[head * band : (head + 1) * band] for head in range(HEADS)]
        return jnp.concatenate(
            [
                jnp.where(low, parts[0][:, :half], parts[1][:, :half]),
                jnp.where(low, parts[2][:, half:], parts[3][:, half:]),
            ],
            axis=1,
        )

    key_grad_ref[...] = jnp.zeros_like(key_grad_ref)
    value_grad_ref[...] = jnp.zeros_like(value_grad_ref)
    attended = []
    query_grads = []
    own_end = strip + own_count
    for index, (query_big, upstream) in enumerate(bands):
        up_big = spread(upstream, rows_ok)
        first = (2 + BAND * index - RADIUS) * SPAN
        last = first + deep
        lower, upper = max(first, 0), min(last, own_end + strip)
        key_band = key_ref[lower:upper]
        value_band = value_ref[lower:upper]
        scores = dot(key_band, query_big, 1, 1) * factor + bias[lower - first : upper - first]
        exponent = jnp.exp2(scores - jnp.max(scores, axis=0, keepdims=True))
        prob = exponent * (1.0 / jnp.sum(exponent, axis=0, keepdims=True))
        dots = dot(value_band, up_big, 1, 1)
        mean_dot = jnp.sum(prob * dots, axis=0, keepdims=True)
        weighted = (prob * (dots - mean_dot)).astype(BF16)
        prob = prob.astype(BF16)
        near, far = max(lower, strip), min(upper, own_end)
        key_grad_ref[near - strip : far - strip] += dot(weighted[near - lower : far - lower], query_big)
        value_grad_ref[near - strip : far - strip] += dot(prob[near - lower : far - lower], up_big)
        if index in (1, 2):
            attended.append(merge(dot(prob, value_band, 0, 0)))
            query_grads.append(merge(dot(weighted, key_band, 0, 0)))

    row = row_in(own_count)
    own_rows = row < 16
    key_rows = own_rows | (top & (row >= SPAN - RADIUS)) | (bottom & (row >= 16) & (row < 16 + RADIUS))
    query_grad = jnp.concatenate(query_grads, axis=0) * head_factor
    raw_query = head_back(query_grad, queries, own_query_recip_ref[...], group)
    raw_key = head_back(key_grad_ref[...] * head_factor, own_key_ref[...], own_key_recip_ref[...], group)
    projected_grad = jnp.concatenate(
        [
            jnp.where(own_rows, raw_query, 0.0),
            jnp.where(key_rows, raw_key, 0.0),
            jnp.where(key_rows, value_grad_ref[...], 0.0),
        ],
        axis=1,
    ).astype(BF16)
    unit, normed = own_unit_ref[...], own_normed_ref[...]
    reciprocal = own_scale_ref[:, :1]
    normed_grad = dot(projected_grad, weight, 1, 1)
    gain_grad = jnp.sum(normed_grad * unit, axis=0, keepdims=True)
    scaled = normed_grad * gain
    token_part = reciprocal * (scaled - unit * jnp.mean(scaled * unit, axis=-1, keepdims=True))
    token_ref[...] = (own_grad.astype(F32) + token_part).astype(BF16)
    attended = jnp.where(own_rows, jnp.concatenate(attended, axis=0), 0.0).astype(BF16)
    weight_grad = dot(projected_grad, normed, 0, 0)
    proj_grad = dot(own_grad, attended, 0, 0)
    for block in range(width // LANES):
        at = slice(block * LANES, (block + 1) * LANES)
        weight_grad_ref[block] = weight_grad[:, at]
        proj_grad_ref[block] = proj_grad[:, at]
    blocks, rows = chunk_ref.shape[:2]
    group = (rows - TAIL) // 8
    for peer in range(blocks):
        line, side = peer // 2, peer % 2
        for part in range(4):
            for block in range(width // LANES):
                if part < 3:
                    start = 6 * group * line + 3 * side + part
                    cells = weight_grad_ref.at[block][pl.ds(start, group, stride=6), :]
                else:
                    start = 2 * group * line + side
                    cells = proj_grad_ref.at[block][pl.ds(start, group, stride=2), :]
                at = (2 * part + block) * group
                chunk_ref[peer, at : at + group] = cells.astype(BF16)
        lanes = gain_grad[:, 2 * group * line // LANES * LANES :][:, :LANES]
        chunk_ref[peer, rows - TAIL :] = jnp.broadcast_to(lanes, (TAIL, LANES)).astype(BF16)


def middle_kernel(chunk_ref, part_ref, sum_ref):
    group = sum_ref.shape[0] // 8
    copies = part_ref.shape[0] // group
    total = sum(chunk_ref[peer].astype(F32) for peer in range(chunk_ref.shape[0]))
    sum_ref[...] = total[: 8 * group]
    gains = total[8 * group : 8 * group + TAIL - 8]
    for column in range(group):
        rows = jnp.concatenate([sum_ref[pl.ds(column, 8, stride=group), :], gains], axis=0).astype(BF16)
        for copy in range(copies):
            part_ref[copies * column + copy] = rows


def final_kernel(scale, place_ref, parts_ref, qkv_ref, proj_ref, gain_ref):
    total = parts_ref[...] * scale
    lane = lax.broadcasted_iota(jnp.int32, (1, LANES), 1)
    gains = []
    for side in range(2):
        for part in range(4):
            at = side * TAIL + 2 * part
            row = jnp.concatenate([total[at : at + 1], total[at + 1 : at + 2]], axis=1)
            if part < 3:
                qkv_ref[3 * side + part : 3 * side + part + 1, :] = row
            else:
                proj_ref[side : side + 1, :] = row
        here = lane == 2 * place_ref[0] % LANES + side
        gains.append(jnp.sum(jnp.where(here, total[at + 2 : at + 3], 0.0), axis=1, keepdims=True))
    gain_ref[...] = jnp.concatenate(gains, axis=1)


def on_device(tokens, edge_tokens, output_grad, norm_gain, qkv_weight, out_weight, head_scale):
    row_count, col_count, width = tokens.shape
    row_devices = lax.axis_size(ROWS)
    col_devices = lax.axis_size(COLS)
    place = lax.axis_index(ROWS)
    grad_scale = (row_count * row_devices * col_count * col_devices) ** (-0.5)
    parity = lax.axis_index(COLS) & 1
    strips = jnp.concatenate(
        [
            tokens[:REACH],
            tokens[row_count - REACH :],
            output_grad[:RADIUS],
            output_grad[row_count - RADIUS :],
        ],
        axis=0,
    )
    strips, edge_tokens = lax.optimization_barrier((lax.all_gather(strips, ROWS, axis=0), edge_tokens))
    strips = strips.transpose(0, 2, 1, 3)
    above = strips[jnp.maximum(place - 1, 0)]
    below = strips[jnp.minimum(place + 1, row_devices - 1)]
    own = tokens.transpose(1, 0, 2)
    grad = output_grad.transpose(1, 0, 2)
    edges = edge_tokens.transpose(2, 0, 1, 3)
    blank = jnp.zeros((col_count, RADIUS, width), BF16)
    upper = jnp.where(
        place == 0, jnp.concatenate([blank, edges[:, 0]], axis=1), above[:, REACH : 2 * REACH]
    )
    lower = jnp.where(
        place == row_devices - 1, jnp.concatenate([edges[:, 1], blank], axis=1), below[:, :REACH]
    )
    gap = jnp.zeros((col_count, SPAN - row_count - 2 * REACH, width), BF16)
    slab = jnp.concatenate([own, lower, gap, upper], axis=1)
    grad_gap = jnp.zeros((col_count, SPAN - row_count - 2 * RADIUS, width), BF16)
    grad_slab = jnp.concatenate(
        [
            grad,
            below[:, 2 * REACH : 2 * REACH + RADIUS],
            grad_gap,
            above[:, 2 * REACH + RADIUS :],
        ],
        axis=1,
    )
    facing_west = jnp.concatenate([slab[:REACH], grad_slab[:RADIUS]], axis=0)
    facing_east = jnp.concatenate([slab[col_count - REACH :], grad_slab[col_count - RADIUS :]], axis=0)
    first = [i for i in range(1, col_devices, 2)]
    pairs = [(i, (i + 1) % col_devices) for i in first]
    odd = lax.ppermute(
        jnp.where(parity == 0, facing_west, facing_east), COLS, pairs + [(b, a) for a, b in pairs]
    )
    even = lax.all_gather(
        jnp.where(parity == 0, facing_east, facing_west),
        COLS,
        axis=0,
        axis_index_groups=[[i, i + 1] for i in range(0, col_devices, 2)],
    )
    cells = col_count * SPAN
    lines = lax.axis_size("x")
    group = col_devices // lines
    whole = pl.BlockSpec(memory_space=pltpu.VMEM)
    scalars = pl.BlockSpec(memory_space=pltpu.SMEM)
    even, slab, grad_slab = lax.optimization_barrier((even, slab, grad_slab))
    wide = jax.ShapeDtypeStruct((cells, width), F32)
    narrow = jax.ShapeDtypeStruct((cells, width), BF16)
    own_parts = pl.pallas_call(
        own_kernel,
        out_shape=(
            jax.ShapeDtypeStruct((8, width), F32),
            wide,
            jax.ShapeDtypeStruct((cells, LANES), F32),
            narrow,
            wide,
            wide,
            narrow,
            narrow,
            wide,
            wide,
            wide,
        ),
        in_specs=[whole] * 6,
        out_specs=(whole,) * 11,
        compiler_params=pltpu.CompilerParams(vmem_limit_bytes=16 * 2**20),
    )(
        head_scale[None, :],
        slab.reshape(cells, width),
        grad_slab.reshape(cells, width),
        norm_gain[None, :],
        qkv_weight,
        out_weight,
    )
    token_grad, chunks = pl.pallas_call(
        block_kernel,
        out_shape=(
            jax.ShapeDtypeStruct((cells, width), BF16),
            jax.ShapeDtypeStruct((2 * lines, 8 * group + TAIL, LANES), BF16),
        ),
        in_specs=[scalars] + [whole] * 17,
        out_specs=(whole,) * 2,
        scratch_shapes=[
            pltpu.VMEM((cells + 2 * REACH * SPAN, width), BF16),
            pltpu.VMEM((cells + 2 * REACH * SPAN, width), BF16),
            pltpu.VMEM((cells, width), F32),
            pltpu.VMEM((cells, width), F32),
            pltpu.VMEM((width // LANES, 3 * width, LANES), F32),
            pltpu.VMEM((width // LANES, width, LANES), F32),
        ],
        compiler_params=pltpu.CompilerParams(vmem_limit_bytes=40 * 2**20),
    )(
        jnp.stack([place, row_devices, parity]).astype(jnp.int32),
        grad_slab.reshape(cells, width),
        odd.reshape(-1, width),
        even.reshape(2, -1, width),
        norm_gain[None, :],
        qkv_weight,
        out_weight,
        *own_parts,
    )
    token_grad = token_grad.reshape(col_count, SPAN, width)[:, :row_count].transpose(1, 0, 2)
    chunks = lax.all_to_all(chunks, ("x", "c"), 0, 0)
    halves = lax.axis_size("h")
    part = pl.pallas_call(
        middle_kernel,
        out_shape=jax.ShapeDtypeStruct((halves * group, TAIL, LANES), BF16),
        in_specs=[whole],
        out_specs=whole,
        scratch_shapes=[pltpu.VMEM((8 * group, LANES), F32)],
        compiler_params=pltpu.CompilerParams(vmem_limit_bytes=8 * 2**20),
    )(chunks)
    part = jnp.sum(lax.all_to_all(part, ("l", "y", "h"), 0, 0).astype(F32), axis=0)
    qkv_grad, proj_grad, gain_grad = pl.pallas_call(
        functools.partial(final_kernel, grad_scale),
        out_shape=(
            jax.ShapeDtypeStruct((6, width), F32),
            jax.ShapeDtypeStruct((2, width), F32),
            jax.ShapeDtypeStruct((1, 2), F32),
        ),
        in_specs=[scalars, whole],
        out_specs=(whole,) * 3,
        compiler_params=pltpu.CompilerParams(vmem_limit_bytes=4 * 2**20),
    )(lax.axis_index(COLS)[None].astype(jnp.int32), lax.all_gather(part, "c", axis=0, tiled=True))
    return token_grad, qkv_grad.T, proj_grad.T, gain_grad.reshape(2)


def solution(mesh):
    parts = SPLIT + (2, 2)
    fine = jax.sharding.Mesh(mesh.devices.reshape(parts), COLS + ROWS)
    return jax.shard_map(
        on_device,
        mesh=fine,
        in_specs=(
            P(ROWS, COLS, None),
            P(None, None, COLS, None),
            P(ROWS, COLS, None),
            P(),
            P(),
            P(),
            P(),
        ),
        out_specs=(P(ROWS, COLS, None), P(None, COLS), P(None, COLS), P(COLS)),
        check_vma=False,
    )
```

```python
import functools
import math

import jax
import jax.numpy as jnp
from jax import lax
from jax.experimental import pallas as pl
from jax.experimental.pallas import tpu as pltpu
from jax.sharding import PartitionSpec as P

HEAD_DIM = 64
HEADS = 4
RADIUS = 3
EPSILON = 1e-06

SPAN = 32
REACH = 2 * RADIUS
BAND = 4
LANES = 128
TAIL = 16
COLS = ("x", "l", "u", "v")
ROWS = ("h", "c")
SPLIT = (4, 4, 4, 2)
LOWEST = -1e30
F32 = jnp.float32
BF16 = jnp.bfloat16


def dot(left, right, left_dim=1, right_dim=0):
    return lax.dot_general(
        left, right, (((left_dim,), (right_dim,)), ((), ())), preferred_element_type=F32
    )


def head_mean(values, group):
    high = values.astype(BF16)
    low = (values - high.astype(F32)).astype(BF16)
    return (dot(high, group) + dot(low, group)) * (1.0 / HEAD_DIM)


def unit_norm(cells):
    rows = cells.astype(F32)
    reciprocal = lax.rsqrt(jnp.mean(rows * rows, axis=-1, keepdims=True) + EPSILON)
    return rows * reciprocal, reciprocal


def head_norm(raw, group):
    reciprocal = lax.rsqrt(head_mean(raw * raw, group) + EPSILON)
    return raw * reciprocal, reciprocal


def head_back(grad, hat, reciprocal, group):
    return reciprocal * (grad - hat * head_mean(grad * hat, group))


def head_group(width):
    head = lax.broadcasted_iota(jnp.int32, (width, width), 0) // HEAD_DIM
    return (head == lax.broadcasted_iota(jnp.int32, (width, width), 1) // HEAD_DIM).astype(BF16)


def own_kernel(
    head_ref, own_ref, own_grad_ref, gain_ref, qkv_ref, out_ref,
    factor_ref, unit_ref, scale_ref, normed_ref, key_ref, key_recip_ref, key_b_ref, value_b_ref, query_ref, query_recip_ref, up_ref,
):
    width = own_ref.shape[1]
    lane = lax.broadcasted_iota(jnp.int32, (1, width), 1) // HEAD_DIM
    factor_ref[...] = jnp.zeros_like(factor_ref)
    for head in range(HEADS):
        factor = jnp.broadcast_to(head_ref[:, head : head + 1] * (1.0 / HEAD_DIM), (1, width))
        factor_ref[:1] = jnp.where(lane == head, factor, factor_ref[:1])
    weight = qkv_ref[...]
    group = head_group(width)
    unit, reciprocal = unit_norm(own_ref[...])
    normed = (unit * gain_ref[...]).astype(BF16)
    keys, key_recip = head_norm(dot(normed, weight[:, width : 2 * width]), group)
    queries, query_recip = head_norm(dot(normed, weight[:, :width]), group)
    unit_ref[...] = unit
    scale_ref[...] = jnp.broadcast_to(reciprocal, scale_ref.shape)
    normed_ref[...] = normed
    key_ref[...] = keys
    key_recip_ref[...] = key_recip
    key_b_ref[...] = keys.astype(BF16)
    value_b_ref[...] = dot(normed, weight[:, 2 * width :]).astype(BF16)
    query_ref[...] = queries
    query_recip_ref[...] = query_recip
    up_ref[...] = dot(own_grad_ref[...], out_ref[...], 1, 1)


def block_kernel(
    lowers,
    place_ref, own_grad_ref, odd_ref, even_ref, gain_ref, qkv_ref, out_ref,
    factor_ref, own_unit_ref, own_scale_ref, own_normed_ref, own_key_ref, own_key_recip_ref, own_key_b_ref, own_value_b_ref,
    own_query_ref, own_query_recip_ref, own_up_ref,
    token_ref, chunk_ref,
    key_ref, value_ref, key_grad_ref, value_grad_ref, weight_grad_ref, proj_grad_ref,
):
    own_count, width = own_grad_ref.shape
    strip = REACH * SPAN
    top = place_ref[0] == 0
    bottom = place_ref[0] == place_ref[1] - 1
    parity = place_ref[2]
    odd_strip, even_strip = odd_ref[...], even_ref[1 - parity]
    west = jnp.where(parity == 0, odd_strip, even_strip)
    east = jnp.where(parity == 0, even_strip, odd_strip)
    gain = gain_ref[...]
    weight = qkv_ref[...]
    group = head_group(width)

    def row_in(count):
        return lax.broadcasted_iota(jnp.int32, (count, 1), 0) & (SPAN - 1)

    def query_rows(count):
        row = row_in(count)
        own = row < 16
        below = (row >= 16) & (row < 16 + RADIUS) & jnp.logical_not(bottom)
        above = (row >= SPAN - RADIUS) & jnp.logical_not(top)
        return own | below | above

    def keys_of(cells, start):
        unit, reciprocal = unit_norm(cells)
        normed = (unit * gain).astype(BF16)
        keys, key_recip = head_norm(dot(normed, weight[:, width : 2 * width]), group)
        values = dot(normed, weight[:, 2 * width :])
        key_ref[start : start + cells.shape[0]] = keys.astype(BF16)
        value_ref[start : start + cells.shape[0]] = values.astype(BF16)
        return normed

    def queries_of(normed):
        return head_norm(dot(normed, weight[:, :width]), group)

    key_ref[strip : strip + own_count] = own_key_b_ref[...]
    value_ref[strip : strip + own_count] = own_value_b_ref[...]
    queries = own_query_ref[...]
    west_normed = keys_of(west[:strip], 0)
    east_normed = keys_of(east[:strip], strip + own_count)
    band = BAND * SPAN
    west_query = queries_of(west_normed[strip - band :])[0]
    east_query = queries_of(east_normed[:band])[0]

    own_grad = own_grad_ref[...]
    out_weight = out_ref[...]
    own_up = own_up_ref[...]
    west_up = dot(west[strip:], out_weight, 1, 1)
    east_up = dot(east[strip:], out_weight, 1, 1)
    empty = jnp.zeros((SPAN, width), F32)

    lane = lax.broadcasted_iota(jnp.int32, (1, width), 1) // HEAD_DIM
    zero = jnp.zeros((), BF16)

    def spread(cells, valid):
        cells = jnp.where(valid, cells, 0.0).astype(BF16)
        return jnp.concatenate([jnp.where(lane == head, cells, zero) for head in range(HEADS)], axis=0)

    rows_ok = query_rows(band)
    strip_col = lax.broadcasted_iota(jnp.int32, (band, 1), 0) // SPAN
    bands = (
        (spread(west_query, rows_ok & (strip_col > 0)), jnp.concatenate([empty, west_up], axis=0)),
        (spread(queries[:band], rows_ok), own_up[:band]),
        (spread(queries[band:], rows_ok), own_up[band:]),
        (spread(east_query, rows_ok & (strip_col < RADIUS)), jnp.concatenate([east_up, empty], axis=0)),
    )

    deep = (BAND + REACH) * SPAN
    key_at = lax.broadcasted_iota(jnp.int32, (deep, band), 0)
    query_at = lax.broadcasted_iota(jnp.int32, (deep, band), 1)
    col_gap = key_at // SPAN - query_at // SPAN
    row_gap = (key_at - query_at + RADIUS) & (SPAN - 1)
    inside = (col_gap >= 0) & (col_gap <= REACH) & (row_gap <= REACH)
    bias = jnp.where(inside, 0.0, LOWEST)
    bias = jnp.concatenate([bias] * HEADS, axis=1)
    head_factor = factor_ref[:1]
    factor = jnp.concatenate(
        [
            jnp.broadcast_to(head_factor[:, head * HEAD_DIM : head * HEAD_DIM + 1], (1, band))
            for head in range(HEADS)
        ],
        axis=1,
    ) * math.log2(math.e)

    def merge(stacked):
        half = width // 2
        low = lax.broadcasted_iota(jnp.int32, (1, half), 1) < HEAD_DIM
        parts = [stacked[head * band : (head + 1) * band] for head in range(HEADS)]
        return jnp.concatenate(
            [
                jnp.where(low, parts[0][:, :half], parts[1][:, :half]),
                jnp.where(low, parts[2][:, half:], parts[3][:, half:]),
            ],
            axis=1,
        )

    key_grad_ref[...] = jnp.zeros_like(key_grad_ref)
    value_grad_ref[...] = jnp.zeros_like(value_grad_ref)
    attended = []
    query_grads = []
    own_end = strip + own_count
    for index, (query_big, upstream) in enumerate(bands):
        up_big = spread(upstream, rows_ok)
        first = (2 + BAND * index - RADIUS) * SPAN
        last = first + deep
        lower, upper = max(first, 0), min(last, own_end + strip)
        key_band = key_ref[lower:upper]
        value_band = value_ref[lower:upper]
        scores = dot(key_band, query_big, 1, 1) * factor + bias[lower - first : upper - first]
        exponent = jnp.exp2(scores - jnp.max(scores, axis=0, keepdims=True))
        prob = exponent * (1.0 / jnp.sum(exponent, axis=0, keepdims=True))
        dots = dot(value_band, up_big, 1, 1)
        mean_dot = jnp.sum(prob * dots, axis=0, keepdims=True)
        weighted = (prob * (dots - mean_dot)).astype(BF16)
        prob = prob.astype(BF16)
        near, far = max(lower, strip), min(upper, own_end)
        key_grad_ref[near - strip : far - strip] += dot(weighted[near - lower : far - lower], query_big)
        value_grad_ref[near - strip : far - strip] += dot(prob[near - lower : far - lower], up_big)
        if index in (1, 2):
            attended.append(merge(dot(prob, value_band, 0, 0)))
            query_grads.append(merge(dot(weighted, key_band, 0, 0)))

    row = row_in(own_count)
    own_rows = row < 16
    key_rows = own_rows | (top & (row >= SPAN - RADIUS)) | (bottom & (row >= 16) & (row < 16 + RADIUS))
    query_grad = jnp.concatenate(query_grads, axis=0) * head_factor
    raw_query = head_back(query_grad, queries, own_query_recip_ref[...], group)
    raw_key = head_back(key_grad_ref[...] * head_factor, own_key_ref[...], own_key_recip_ref[...], group)
    projected_grad = jnp.concatenate(
        [
            jnp.where(own_rows, raw_query, 0.0),
            jnp.where(key_rows, raw_key, 0.0),
            jnp.where(key_rows, value_grad_ref[...], 0.0),
        ],
        axis=1,
    ).astype(BF16)
    unit, normed = own_unit_ref[...], own_normed_ref[...]
    reciprocal = own_scale_ref[:, :1]
    normed_grad = dot(projected_grad, weight, 1, 1)
    gain_grad = jnp.sum(normed_grad * unit, axis=0, keepdims=True)
    scaled = normed_grad * gain
    token_part = reciprocal * (scaled - unit * jnp.mean(scaled * unit, axis=-1, keepdims=True))
    token_ref[...] = (own_grad.astype(F32) + token_part).astype(BF16)
    attended = jnp.where(own_rows, jnp.concatenate(attended, axis=0), 0.0).astype(BF16)
    weight_grad = dot(projected_grad, normed, 0, 0)
    proj_grad = dot(own_grad, attended, 0, 0)
    for block in range(width // LANES):
        at = slice(block * LANES, (block + 1) * LANES)
        weight_grad_ref[block] = weight_grad[:, at]
        proj_grad_ref[block] = proj_grad[:, at]
    peers, rows = chunk_ref.shape[:2]
    group = (rows - TAIL) // 8
    for peer in range(peers):
        line, lower, side = peer // (2 * lowers), peer // 2 % lowers, peer % 2
        column = line * group * lowers + lower
        for part in range(4):
            for block in range(width // LANES):
                if part < 3:
                    cells_ref, start, stride = weight_grad_ref, 6 * column + 3 * side + part, 6 * lowers
                else:
                    cells_ref, start, stride = proj_grad_ref, 2 * column + side, 2 * lowers
                at = (2 * part + block) * group
                cells = cells_ref.at[block][pl.ds(start, group, stride=stride), :]
                chunk_ref[peer, at : at + group] = cells.astype(BF16)
        lanes = gain_grad[:, 2 * column // LANES * LANES :][:, :LANES]
        chunk_ref[peer, rows - TAIL :] = jnp.broadcast_to(lanes, (TAIL, LANES)).astype(BF16)


def middle_kernel(chunk_ref, part_ref, sum_ref):
    group = sum_ref.shape[0] // 8
    copies = part_ref.shape[0] // group
    total = sum(chunk_ref[peer].astype(F32) for peer in range(chunk_ref.shape[0]))
    sum_ref[...] = total[: 8 * group]
    gains = total[8 * group : 8 * group + TAIL - 8]
    for column in range(group):
        rows = jnp.concatenate([sum_ref[pl.ds(column, 8, stride=group), :], gains], axis=0).astype(BF16)
        for copy in range(copies):
            part_ref[copies * column + copy] = rows


def final_kernel(scale, place_ref, parts_ref, qkv_ref, proj_ref, gain_ref):
    total = parts_ref[...] * scale
    lane = lax.broadcasted_iota(jnp.int32, (1, LANES), 1)
    gains = []
    for side in range(2):
        for part in range(4):
            at = side * TAIL + 2 * part
            row = jnp.concatenate([total[at : at + 1], total[at + 1 : at + 2]], axis=1)
            if part < 3:
                qkv_ref[3 * side + part : 3 * side + part + 1, :] = row
            else:
                proj_ref[side : side + 1, :] = row
        here = lane == 2 * place_ref[0] % LANES + side
        gains.append(jnp.sum(jnp.where(here, total[at + 2 : at + 3], 0.0), axis=1, keepdims=True))
    gain_ref[...] = jnp.concatenate(gains, axis=1)


def on_device(tokens, edge_tokens, output_grad, norm_gain, qkv_weight, out_weight, head_scale):
    row_count, col_count, width = tokens.shape
    row_devices = lax.axis_size(ROWS)
    col_devices = lax.axis_size(COLS)
    place = lax.axis_index(ROWS)
    grad_scale = (row_count * row_devices * col_count * col_devices) ** (-0.5)
    parity = lax.axis_index(COLS) & 1
    strips = jnp.concatenate(
        [
            tokens[:REACH],
            tokens[row_count - REACH :],
            output_grad[:RADIUS],
            output_grad[row_count - RADIUS :],
        ],
        axis=0,
    )
    strips, edge_tokens = lax.optimization_barrier((lax.all_gather(strips, ROWS, axis=0), edge_tokens))
    strips = strips.transpose(0, 2, 1, 3)
    above = strips[jnp.maximum(place - 1, 0)]
    below = strips[jnp.minimum(place + 1, row_devices - 1)]
    own = tokens.transpose(1, 0, 2)
    grad = output_grad.transpose(1, 0, 2)
    edges = edge_tokens.transpose(2, 0, 1, 3)
    blank = jnp.zeros((col_count, RADIUS, width), BF16)
    upper = jnp.where(
        place == 0, jnp.concatenate([blank, edges[:, 0]], axis=1), above[:, REACH : 2 * REACH]
    )
    lower = jnp.where(
        place == row_devices - 1, jnp.concatenate([edges[:, 1], blank], axis=1), below[:, :REACH]
    )
    gap = jnp.zeros((col_count, SPAN - row_count - 2 * REACH, width), BF16)
    slab = jnp.concatenate([own, lower, gap, upper], axis=1)
    grad_gap = jnp.zeros((col_count, SPAN - row_count - 2 * RADIUS, width), BF16)
    grad_slab = jnp.concatenate(
        [
            grad,
            below[:, 2 * REACH : 2 * REACH + RADIUS],
            grad_gap,
            above[:, 2 * REACH + RADIUS :],
        ],
        axis=1,
    )
    facing_west = jnp.concatenate([slab[:REACH], grad_slab[:RADIUS]], axis=0)
    facing_east = jnp.concatenate([slab[col_count - REACH :], grad_slab[col_count - RADIUS :]], axis=0)
    first = [i for i in range(1, col_devices, 2)]
    pairs = [(i, (i + 1) % col_devices) for i in first]
    odd = lax.ppermute(
        jnp.where(parity == 0, facing_west, facing_east), COLS, pairs + [(b, a) for a, b in pairs]
    )
    even = lax.all_gather(
        jnp.where(parity == 0, facing_east, facing_west),
        COLS,
        axis=0,
        axis_index_groups=[[i, i + 1] for i in range(0, col_devices, 2)],
    )
    cells = col_count * SPAN
    lowers = lax.axis_size("v")
    peers = 2 * lax.axis_size("x") * lowers
    group = 2 * col_devices // peers
    whole = pl.BlockSpec(memory_space=pltpu.VMEM)
    scalars = pl.BlockSpec(memory_space=pltpu.SMEM)
    even, slab, grad_slab = lax.optimization_barrier((even, slab, grad_slab))
    wide = jax.ShapeDtypeStruct((cells, width), F32)
    narrow = jax.ShapeDtypeStruct((cells, width), BF16)
    own_parts = pl.pallas_call(
        own_kernel,
        out_shape=(
            jax.ShapeDtypeStruct((8, width), F32),
            wide,
            jax.ShapeDtypeStruct((cells, LANES), F32),
            narrow,
            wide,
            wide,
            narrow,
            narrow,
            wide,
            wide,
            wide,
        ),
        in_specs=[whole] * 6,
        out_specs=(whole,) * 11,
        compiler_params=pltpu.CompilerParams(vmem_limit_bytes=16 * 2**20),
    )(
        head_scale[None, :],
        slab.reshape(cells, width),
        grad_slab.reshape(cells, width),
        norm_gain[None, :],
        qkv_weight,
        out_weight,
    )
    token_grad, chunks = pl.pallas_call(
        functools.partial(block_kernel, lowers),
        out_shape=(
            jax.ShapeDtypeStruct((cells, width), BF16),
            jax.ShapeDtypeStruct((peers, 8 * group + TAIL, LANES), BF16),
        ),
        in_specs=[scalars] + [whole] * 17,
        out_specs=(whole,) * 2,
        scratch_shapes=[
            pltpu.VMEM((cells + 2 * REACH * SPAN, width), BF16),
            pltpu.VMEM((cells + 2 * REACH * SPAN, width), BF16),
            pltpu.VMEM((cells, width), F32),
            pltpu.VMEM((cells, width), F32),
            pltpu.VMEM((width // LANES, 3 * width, LANES), F32),
            pltpu.VMEM((width // LANES, width, LANES), F32),
        ],
        compiler_params=pltpu.CompilerParams(vmem_limit_bytes=40 * 2**20),
    )(
        jnp.stack([place, row_devices, parity]).astype(jnp.int32),
        grad_slab.reshape(cells, width),
        odd.reshape(-1, width),
        even.reshape(2, -1, width),
        norm_gain[None, :],
        qkv_weight,
        out_weight,
        *own_parts,
    )
    token_grad = token_grad.reshape(col_count, SPAN, width)[:, :row_count].transpose(1, 0, 2)
    chunks = lax.all_to_all(chunks, ("x", "v", "c"), 0, 0)
    halves = lax.axis_size("h")
    part = pl.pallas_call(
        middle_kernel,
        out_shape=jax.ShapeDtypeStruct((halves * group, TAIL, LANES), BF16),
        in_specs=[whole],
        out_specs=whole,
        scratch_shapes=[pltpu.VMEM((8 * group, LANES), F32)],
        compiler_params=pltpu.CompilerParams(vmem_limit_bytes=8 * 2**20),
    )(chunks)
    part = jnp.sum(lax.all_to_all(part, ("l", "u", "h"), 0, 0).astype(F32), axis=0)
    qkv_grad, proj_grad, gain_grad = pl.pallas_call(
        functools.partial(final_kernel, grad_scale),
        out_shape=(
            jax.ShapeDtypeStruct((6, width), F32),
            jax.ShapeDtypeStruct((2, width), F32),
            jax.ShapeDtypeStruct((1, 2), F32),
        ),
        in_specs=[scalars, whole],
        out_specs=(whole,) * 3,
        compiler_params=pltpu.CompilerParams(vmem_limit_bytes=4 * 2**20),
    )(lax.axis_index(COLS)[None].astype(jnp.int32), lax.all_gather(part, "c", axis=0, tiled=True))
    return token_grad, qkv_grad.T, proj_grad.T, gain_grad.reshape(2)


def solution(mesh):
    parts = SPLIT + (2, 2)
    fine = jax.sharding.Mesh(mesh.devices.reshape(parts), COLS + ROWS)
    return jax.shard_map(
        on_device,
        mesh=fine,
        in_specs=(
            P(ROWS, COLS, None),
            P(None, None, COLS, None),
            P(ROWS, COLS, None),
            P(),
            P(),
            P(),
            P(),
        ),
        out_specs=(P(ROWS, COLS, None), P(None, COLS), P(None, COLS), P(COLS)),
        check_vma=False,
    )
```

```python
import functools
import math

import jax
import jax.numpy as jnp
from jax import lax
from jax.experimental import pallas as pl
from jax.experimental.pallas import tpu as pltpu
from jax.sharding import PartitionSpec as P

HEAD_DIM = 64
HEADS = 4
RADIUS = 3
EPSILON = 1e-06

SPAN = 32
REACH = 2 * RADIUS
BAND = 4
LANES = 128
TAIL = 16
COLS = ("x", "l", "u", "v")
ROWS = ("h", "c")
SPLIT = (4, 4, 4, 2)
LOWEST = -1e30
F32 = jnp.float32
BF16 = jnp.bfloat16


def dot(left, right, left_dim=1, right_dim=0):
    return lax.dot_general(
        left, right, (((left_dim,), (right_dim,)), ((), ())), preferred_element_type=F32
    )


def head_mean(values, group):
    high = values.astype(BF16)
    low = (values - high.astype(F32)).astype(BF16)
    return (dot(high, group) + dot(low, group)) * (1.0 / HEAD_DIM)


def high_low(values, count, first):
    high = values.astype(BF16).astype(F32)
    row = lax.broadcasted_iota(jnp.int32, (count, values.shape[1]), 0)
    low = jnp.where(row == first + 1, values - high, 0.0)
    return jnp.where(row == first, high, low).astype(BF16)


def unit_norm(cells):
    rows = cells.astype(F32)
    reciprocal = lax.rsqrt(jnp.mean(rows * rows, axis=-1, keepdims=True) + EPSILON)
    return rows * reciprocal, reciprocal


def head_norm(raw, group):
    reciprocal = lax.rsqrt(head_mean(raw * raw, group) + EPSILON)
    return raw * reciprocal, reciprocal


def head_back(grad, hat, reciprocal, group):
    return reciprocal * (grad - hat * head_mean(grad * hat, group))


def head_group(width):
    head = lax.broadcasted_iota(jnp.int32, (width, width), 0) // HEAD_DIM
    return (head == lax.broadcasted_iota(jnp.int32, (width, width), 1) // HEAD_DIM).astype(BF16)


def own_kernel(
    own_ref, own_grad_ref, gain_ref, qkv_ref, out_ref,
    unit_ref, scale_ref, normed_ref, key_ref, key_recip_ref, key_b_ref, value_b_ref, query_ref, query_recip_ref, up_ref,
):
    width = own_ref.shape[1]
    weight = qkv_ref[...]
    group = head_group(width)
    unit, reciprocal = unit_norm(own_ref[...])
    normed = (unit * gain_ref[:, :width]).astype(BF16)
    keys, key_recip = head_norm(dot(normed, weight[:, width : 2 * width]), group)
    queries, query_recip = head_norm(dot(normed, weight[:, :width]), group)
    unit_ref[...] = unit
    scale_ref[...] = jnp.broadcast_to(reciprocal, scale_ref.shape)
    normed_ref[...] = normed
    key_ref[...] = keys
    key_recip_ref[...] = key_recip
    key_b_ref[...] = keys.astype(BF16)
    value_b_ref[...] = dot(normed, weight[:, 2 * width :]).astype(BF16)
    query_ref[...] = queries
    query_recip_ref[...] = query_recip
    up_ref[...] = dot(own_grad_ref[...], out_ref[...], 1, 1)


def block_kernel(
    lowers,
    place_ref, own_grad_ref, odd_ref, even_ref, gain_ref, qkv_ref, out_ref,
    own_unit_ref, own_scale_ref, own_normed_ref, own_key_ref, own_key_recip_ref, own_key_b_ref, own_value_b_ref,
    own_query_ref, own_query_recip_ref, own_up_ref,
    token_ref, chunk_ref,
    key_ref, value_ref, key_grad_ref, value_grad_ref, weight_grad_ref, proj_grad_ref,
):
    own_count, width = own_grad_ref.shape
    strip = REACH * SPAN
    top = place_ref[0] == 0
    bottom = place_ref[0] == place_ref[1] - 1
    parity = place_ref[2]
    odd_strip, even_strip = odd_ref[...], even_ref[1 - parity]
    west = jnp.where(parity == 0, odd_strip, even_strip)
    east = jnp.where(parity == 0, even_strip, odd_strip)
    gain = gain_ref[:, :width]
    weight = qkv_ref[...]
    group = head_group(width)

    def row_in(count):
        return lax.broadcasted_iota(jnp.int32, (count, 1), 0) & (SPAN - 1)

    def query_rows(count):
        row = row_in(count)
        own = row < 16
        below = (row >= 16) & (row < 16 + RADIUS) & jnp.logical_not(bottom)
        above = (row >= SPAN - RADIUS) & jnp.logical_not(top)
        return own | below | above

    def keys_of(cells, start):
        unit, reciprocal = unit_norm(cells)
        normed = (unit * gain).astype(BF16)
        keys, key_recip = head_norm(dot(normed, weight[:, width : 2 * width]), group)
        values = dot(normed, weight[:, 2 * width :])
        key_ref[start : start + cells.shape[0]] = keys.astype(BF16)
        value_ref[start : start + cells.shape[0]] = values.astype(BF16)
        return normed

    def queries_of(normed):
        return head_norm(dot(normed, weight[:, :width]), group)

    key_ref[strip : strip + own_count] = own_key_b_ref[...]
    value_ref[strip : strip + own_count] = own_value_b_ref[...]
    queries = own_query_ref[...]
    west_normed = keys_of(west[:strip], 0)
    east_normed = keys_of(east[:strip], strip + own_count)
    band = BAND * SPAN
    west_query = queries_of(west_normed[strip - band :])[0]
    east_query = queries_of(east_normed[:band])[0]

    own_grad = own_grad_ref[...]
    out_weight = out_ref[...]
    own_up = own_up_ref[...]
    west_up = dot(west[strip:], out_weight, 1, 1)
    east_up = dot(east[strip:], out_weight, 1, 1)
    empty = jnp.zeros((SPAN, width), F32)

    lane = lax.broadcasted_iota(jnp.int32, (1, width), 1) // HEAD_DIM
    zero = jnp.zeros((), BF16)

    def spread(cells, valid):
        cells = jnp.where(valid, cells, 0.0).astype(BF16)
        return jnp.concatenate([jnp.where(lane == head, cells, zero) for head in range(HEADS)], axis=0)

    rows_ok = query_rows(band)
    strip_col = lax.broadcasted_iota(jnp.int32, (band, 1), 0) // SPAN
    bands = (
        (spread(west_query, rows_ok & (strip_col > 0)), jnp.concatenate([empty, west_up], axis=0)),
        (spread(queries[:band], rows_ok), own_up[:band]),
        (spread(queries[band:], rows_ok), own_up[band:]),
        (spread(east_query, rows_ok & (strip_col < RADIUS)), jnp.concatenate([east_up, empty], axis=0)),
    )

    deep = (BAND + REACH) * SPAN
    key_at = lax.broadcasted_iota(jnp.int32, (deep, band), 0)
    query_at = lax.broadcasted_iota(jnp.int32, (deep, band), 1)
    col_gap = key_at // SPAN - query_at // SPAN
    row_gap = (key_at - query_at + RADIUS) & (SPAN - 1)
    inside = (col_gap >= 0) & (col_gap <= REACH) & (row_gap <= REACH)
    bias = jnp.where(inside, 0.0, LOWEST)
    bias = jnp.concatenate([bias] * HEADS, axis=1)
    lane_factors = [gain_ref[:, width + head : width + head + 1] * (1.0 / HEAD_DIM) for head in range(HEADS)]
    head_factor = jnp.zeros((1, width), F32)
    for head in range(HEADS):
        head_factor = jnp.where(lane == head, jnp.broadcast_to(lane_factors[head], (1, width)), head_factor)
    factor = jnp.concatenate(
        [
            jnp.broadcast_to(lane_factors[head], (1, band)) for head in range(HEADS)
        ],
        axis=1,
    ) * math.log2(math.e)

    def merge(stacked):
        half = width // 2
        low = lax.broadcasted_iota(jnp.int32, (1, half), 1) < HEAD_DIM
        parts = [stacked[head * band : (head + 1) * band] for head in range(HEADS)]
        return jnp.concatenate(
            [
                jnp.where(low, parts[0][:, :half], parts[1][:, :half]),
                jnp.where(low, parts[2][:, half:], parts[3][:, half:]),
            ],
            axis=1,
        )

    key_grad_ref[...] = jnp.zeros_like(key_grad_ref)
    value_grad_ref[...] = jnp.zeros_like(value_grad_ref)
    attended = []
    query_grads = []
    own_end = strip + own_count
    for index, (query_big, upstream) in enumerate(bands):
        up_big = spread(upstream, rows_ok)
        first = (2 + BAND * index - RADIUS) * SPAN
        last = first + deep
        lower, upper = max(first, 0), min(last, own_end + strip)
        key_band = key_ref[lower:upper]
        value_band = value_ref[lower:upper]
        scores = dot(key_band, query_big, 1, 1) * factor + bias[lower - first : upper - first]
        exponent = jnp.exp2(scores - jnp.max(scores, axis=0, keepdims=True))
        prob = exponent * (1.0 / jnp.sum(exponent, axis=0, keepdims=True))
        dots = dot(value_band, up_big, 1, 1)
        mean_dot = jnp.sum(prob * dots, axis=0, keepdims=True)
        weighted = (prob * (dots - mean_dot)).astype(BF16)
        prob = prob.astype(BF16)
        near, far = max(lower, strip), min(upper, own_end)
        key_grad_ref[near - strip : far - strip] += dot(weighted[near - lower : far - lower], query_big)
        value_grad_ref[near - strip : far - strip] += dot(prob[near - lower : far - lower], up_big)
        if index in (1, 2):
            attended.append(merge(dot(prob, value_band, 0, 0)))
            query_grads.append(merge(dot(weighted, key_band, 0, 0)))

    row = row_in(own_count)
    own_rows = row < 16
    key_rows = own_rows | (top & (row >= SPAN - RADIUS)) | (bottom & (row >= 16) & (row < 16 + RADIUS))
    query_grad = jnp.concatenate(query_grads, axis=0) * head_factor
    raw_query = head_back(query_grad, queries, own_query_recip_ref[...], group)
    raw_key = head_back(key_grad_ref[...] * head_factor, own_key_ref[...], own_key_recip_ref[...], group)
    projected_grad = jnp.concatenate(
        [
            jnp.where(own_rows, raw_query, 0.0),
            jnp.where(key_rows, raw_key, 0.0),
            jnp.where(key_rows, value_grad_ref[...], 0.0),
        ],
        axis=1,
    )
    projected_high = projected_grad.astype(BF16)
    projected_low = (projected_grad - projected_high.astype(F32)).astype(BF16)
    unit, normed = own_unit_ref[...], own_normed_ref[...]
    reciprocal = own_scale_ref[:, :1]
    normed_grad = dot(projected_high, weight, 1, 1) + dot(projected_low, weight, 1, 1)
    gain_grad = jnp.sum(normed_grad * unit, axis=0, keepdims=True)
    scaled = normed_grad * gain
    token_part = reciprocal * (scaled - unit * jnp.mean(scaled * unit, axis=-1, keepdims=True))
    token_ref[...] = (own_grad.astype(F32) + token_part).astype(BF16)
    attended = jnp.where(own_rows, jnp.concatenate(attended, axis=0), 0.0).astype(BF16)
    weight_grad = dot(projected_high, normed, 0, 0)
    proj_grad = dot(own_grad, attended, 0, 0)
    for block in range(width // LANES):
        at = slice(block * LANES, (block + 1) * LANES)
        weight_grad_ref[block] = weight_grad[:, at]
        proj_grad_ref[block] = proj_grad[:, at]
    peers, rows = chunk_ref.shape[1:3]
    group = (rows - TAIL) // 8
    for index in range(2 * peers):
        peer, side = index // 2, index % 2
        line, lower = peer // lowers, peer % lowers
        half = (place_ref[0] + side) % 2
        column = line * group * lowers + lower
        for part in range(4):
            for block in range(width // LANES):
                if part < 3:
                    cells_ref, start, stride = weight_grad_ref, 6 * column + 3 * side + part, 6 * lowers
                else:
                    cells_ref, start, stride = proj_grad_ref, 2 * column + side, 2 * lowers
                at = (2 * part + block) * group
                cells = cells_ref.at[block][pl.ds(start, group, stride=stride), :]
                chunk_ref[half, peer, at : at + group] = cells.astype(BF16)
        lanes = gain_grad[:, 2 * column // LANES * LANES :][:, :LANES]
        chunk_ref[half, peer, rows - TAIL :] = high_low(lanes, TAIL, 2 * half)


def middle_kernel(chunk_ref, part_ref, sum_ref):
    group = sum_ref.shape[0] // 8
    copies = part_ref.shape[0] // group
    total = sum(chunk_ref[peer].astype(F32) for peer in range(chunk_ref.shape[0]))
    sum_ref[...] = total[: 8 * group]
    gains = high_low(jnp.sum(total[8 * group :], axis=0, keepdims=True), TAIL - 8, 0).astype(F32)
    for column in range(group):
        rows = jnp.concatenate([sum_ref[pl.ds(column, 8, stride=group), :], gains], axis=0).astype(BF16)
        for copy in range(copies):
            part_ref[copies * column + copy] = rows


def final_kernel(scale, place_ref, parts_ref, qkv_ref, proj_ref, gain_ref):
    total = parts_ref[...] * scale
    lane = lax.broadcasted_iota(jnp.int32, (1, LANES), 1)
    gains = []
    for side in range(2):
        for part in range(4):
            at = side * TAIL + 2 * part
            row = jnp.concatenate([total[at : at + 1], total[at + 1 : at + 2]], axis=1)
            if part < 3:
                qkv_ref[3 * side + part : 3 * side + part + 1, :] = row
            else:
                proj_ref[side : side + 1, :] = row
        here = lane == 2 * place_ref[0] % LANES + side
        gains.append(jnp.sum(jnp.where(here, total[at + 2 : at + 3] + total[at + 3 : at + 4], 0.0), axis=1, keepdims=True))
    gain_ref[...] = jnp.concatenate(gains, axis=1)


def on_device(tokens, edge_tokens, output_grad, norm_gain, qkv_weight, out_weight, head_scale):
    row_count, col_count, width = tokens.shape
    row_devices = lax.axis_size(ROWS)
    col_devices = lax.axis_size(COLS)
    place = lax.axis_index(ROWS)
    grad_scale = (row_count * row_devices * col_count * col_devices) ** (-0.5)
    parity = lax.axis_index(COLS) & 1
    gains = jnp.concatenate([norm_gain, head_scale, jnp.zeros((LANES - HEADS,), F32)])[None, :]
    gains, tokens, output_grad = lax.optimization_barrier((gains, tokens, output_grad))
    strips = jnp.concatenate(
        [
            tokens[:REACH],
            tokens[row_count - REACH :],
            output_grad[:RADIUS],
            output_grad[row_count - RADIUS :],
        ],
        axis=0,
    )
    strips, edge_tokens, tokens, output_grad = lax.optimization_barrier(
        (lax.all_gather(strips, ROWS, axis=0), edge_tokens, tokens, output_grad)
    )
    strips = strips.transpose(0, 2, 1, 3)
    above = strips[jnp.maximum(place - 1, 0)]
    below = strips[jnp.minimum(place + 1, row_devices - 1)]
    own = tokens.transpose(1, 0, 2)
    grad = output_grad.transpose(1, 0, 2)
    edges = edge_tokens.transpose(2, 0, 1, 3)
    blank = jnp.zeros((col_count, RADIUS, width), BF16)
    upper = jnp.where(
        place == 0, jnp.concatenate([blank, edges[:, 0]], axis=1), above[:, REACH : 2 * REACH]
    )
    lower = jnp.where(
        place == row_devices - 1, jnp.concatenate([edges[:, 1], blank], axis=1), below[:, :REACH]
    )
    gap = jnp.zeros((col_count, SPAN - row_count - 2 * REACH, width), BF16)
    slab = jnp.concatenate([own, lower, gap, upper], axis=1)
    grad_gap = jnp.zeros((col_count, SPAN - row_count - 2 * RADIUS, width), BF16)
    grad_slab = jnp.concatenate(
        [
            grad,
            below[:, 2 * REACH : 2 * REACH + RADIUS],
            grad_gap,
            above[:, 2 * REACH + RADIUS :],
        ],
        axis=1,
    )
    facing_west = jnp.concatenate([slab[:REACH], grad_slab[:RADIUS]], axis=0)
    facing_east = jnp.concatenate([slab[col_count - REACH :], grad_slab[col_count - RADIUS :]], axis=0)
    first = [i for i in range(1, col_devices, 2)]
    pairs = [(i, (i + 1) % col_devices) for i in first]
    odd = lax.ppermute(
        jnp.where(parity == 0, facing_west, facing_east), COLS, pairs + [(b, a) for a, b in pairs]
    )
    even = lax.all_gather(
        jnp.where(parity == 0, facing_east, facing_west),
        COLS,
        axis=0,
        axis_index_groups=[[i, i + 1] for i in range(0, col_devices, 2)],
    )
    cells = col_count * SPAN
    lowers = lax.axis_size("v")
    peers = lax.axis_size("x") * lowers
    group = col_devices // peers
    whole = pl.BlockSpec(memory_space=pltpu.VMEM)
    scalars = pl.BlockSpec(memory_space=pltpu.SMEM)
    even, slab, grad_slab = lax.optimization_barrier((even, slab, grad_slab))
    wide = jax.ShapeDtypeStruct((cells, width), F32)
    narrow = jax.ShapeDtypeStruct((cells, width), BF16)
    own_parts = pl.pallas_call(
        own_kernel,
        out_shape=(
            wide,
            jax.ShapeDtypeStruct((cells, LANES), F32),
            narrow,
            wide,
            wide,
            narrow,
            narrow,
            wide,
            wide,
            wide,
        ),
        in_specs=[whole] * 5,
        out_specs=(whole,) * 10,
        compiler_params=pltpu.CompilerParams(vmem_limit_bytes=16 * 2**20),
    )(
        slab.reshape(cells, width),
        grad_slab.reshape(cells, width),
        gains,
        qkv_weight,
        out_weight,
    )
    token_grad, chunks = pl.pallas_call(
        functools.partial(block_kernel, lowers),
        out_shape=(
            jax.ShapeDtypeStruct((cells, width), BF16),
            jax.ShapeDtypeStruct((2, peers, 8 * group + TAIL, LANES), BF16),
        ),
        in_specs=[scalars] + [whole] * 16,
        out_specs=(whole,) * 2,
        scratch_shapes=[
            pltpu.VMEM((cells + 2 * REACH * SPAN, width), BF16),
            pltpu.VMEM((cells + 2 * REACH * SPAN, width), BF16),
            pltpu.VMEM((cells, width), F32),
            pltpu.VMEM((cells, width), F32),
            pltpu.VMEM((width // LANES, 3 * width, LANES), F32),
            pltpu.VMEM((width // LANES, width, LANES), F32),
        ],
        compiler_params=pltpu.CompilerParams(vmem_limit_bytes=40 * 2**20),
    )(
        jnp.stack([place, row_devices, parity]).astype(jnp.int32),
        grad_slab.reshape(cells, width),
        odd.reshape(-1, width),
        even.reshape(2, -1, width),
        gains,
        qkv_weight,
        out_weight,
        *own_parts,
    )
    token_grad = token_grad.reshape(col_count, SPAN, width)[:, :row_count].transpose(1, 0, 2)
    received = lax.all_gather(chunks[1].reshape(-1, LANES), "c", axis=0)[1 - lax.axis_index("c")]
    chunks = (chunks[0].astype(F32) + received.reshape(chunks.shape[1:]).astype(F32)).astype(BF16)
    chunks = lax.all_to_all(chunks, ("x", "v"), 0, 0)
    halves = lax.axis_size("h")
    part = pl.pallas_call(
        middle_kernel,
        out_shape=jax.ShapeDtypeStruct((halves * group, TAIL, LANES), BF16),
        in_specs=[whole],
        out_specs=whole,
        scratch_shapes=[pltpu.VMEM((8 * group, LANES), F32)],
        compiler_params=pltpu.CompilerParams(vmem_limit_bytes=8 * 2**20),
    )(chunks)
    part = jnp.sum(lax.all_to_all(part, ("l", "u", "h"), 0, 0).astype(F32), axis=0)
    qkv_grad, proj_grad, gain_grad = pl.pallas_call(
        functools.partial(final_kernel, grad_scale),
        out_shape=(
            jax.ShapeDtypeStruct((6, width), F32),
            jax.ShapeDtypeStruct((2, width), F32),
            jax.ShapeDtypeStruct((1, 2), F32),
        ),
        in_specs=[scalars, whole],
        out_specs=(whole,) * 3,
        compiler_params=pltpu.CompilerParams(vmem_limit_bytes=4 * 2**20),
    )(lax.axis_index(COLS)[None].astype(jnp.int32), lax.all_gather(part, "c", axis=0, tiled=True))
    return token_grad, qkv_grad.T, proj_grad.T, gain_grad.reshape(2)


def solution(mesh):
    parts = SPLIT + (2, 2)
    fine = jax.sharding.Mesh(mesh.devices.reshape(parts), COLS + ROWS)
    return jax.shard_map(
        on_device,
        mesh=fine,
        in_specs=(
            P(ROWS, COLS, None),
            P(None, None, COLS, None),
            P(ROWS, COLS, None),
            P(),
            P(),
            P(),
            P(),
        ),
        out_specs=(P(ROWS, COLS, None), P(None, COLS), P(None, COLS), P(COLS)),
        check_vma=False,
    )
```

```python
import functools
import math

import jax
import jax.numpy as jnp
from jax import lax
from jax.experimental import pallas as pl
from jax.experimental.pallas import tpu as pltpu
from jax.sharding import PartitionSpec as P

HEAD_DIM = 64
HEADS = 4
RADIUS = 3
EPSILON = 1e-06

SPAN = 32
REACH = 2 * RADIUS
BAND = 4
LANES = 128
TAIL = 16
COLS = ("x", "l", "u", "v")
ROWS = ("h", "c")
SPLIT = (4, 4, 4, 2)
LOWEST = -1e30
F32 = jnp.float32
BF16 = jnp.bfloat16


def dot(left, right, left_dim=1, right_dim=0):
    return lax.dot_general(
        left, right, (((left_dim,), (right_dim,)), ((), ())), preferred_element_type=F32
    )


def head_mean(values, group):
    high = values.astype(BF16)
    low = (values - high.astype(F32)).astype(BF16)
    return (dot(high, group) + dot(low, group)) * (1.0 / HEAD_DIM)


def high_low(values, count, first):
    high = values.astype(BF16).astype(F32)
    row = lax.broadcasted_iota(jnp.int32, (count, values.shape[1]), 0)
    low = jnp.where(row == first + 1, values - high, 0.0)
    return jnp.where(row == first, high, low).astype(BF16)


def unit_norm(cells):
    rows = cells.astype(F32)
    reciprocal = lax.rsqrt(jnp.mean(rows * rows, axis=-1, keepdims=True) + EPSILON)
    return rows * reciprocal, reciprocal


def head_norm(raw, group):
    reciprocal = lax.rsqrt(head_mean(raw * raw, group) + EPSILON)
    return raw * reciprocal, reciprocal


def head_back(grad, hat, reciprocal, group):
    return reciprocal * (grad - hat * head_mean(grad * hat, group))


def head_group(width):
    head = lax.broadcasted_iota(jnp.int32, (width, width), 0) // HEAD_DIM
    return (head == lax.broadcasted_iota(jnp.int32, (width, width), 1) // HEAD_DIM).astype(BF16)


def own_kernel(
    own_ref, own_grad_ref, gain_ref, qkv_ref, out_ref,
    unit_ref, scale_ref, normed_ref, key_ref, key_recip_ref, key_b_ref, value_b_ref, query_ref, query_recip_ref, up_ref,
):
    width = own_ref.shape[1]
    weight = qkv_ref[...]
    group = head_group(width)
    unit, reciprocal = unit_norm(own_ref[...])
    normed = (unit * gain_ref[:, :width]).astype(BF16)
    keys, key_recip = head_norm(dot(normed, weight[:, width : 2 * width]), group)
    queries, query_recip = head_norm(dot(normed, weight[:, :width]), group)
    unit_ref[...] = unit
    scale_ref[...] = jnp.broadcast_to(reciprocal, scale_ref.shape)
    normed_ref[...] = normed
    key_ref[...] = keys
    key_recip_ref[...] = key_recip
    key_b_ref[...] = keys.astype(BF16)
    value_b_ref[...] = dot(normed, weight[:, 2 * width :]).astype(BF16)
    query_ref[...] = queries
    query_recip_ref[...] = query_recip
    up_ref[...] = dot(own_grad_ref[...], out_ref[...], 1, 1)


def block_kernel(
    lowers,
    place_ref, own_grad_ref, odd_ref, even_ref, gain_ref, qkv_ref, out_ref,
    own_unit_ref, own_normed_ref, own_key_ref, own_key_recip_ref, own_key_b_ref, own_value_b_ref,
    own_query_ref, own_query_recip_ref, own_up_ref,
    normed_grad_ref, chunk_ref,
    key_ref, value_ref, key_grad_ref, value_grad_ref, weight_grad_ref, proj_grad_ref,
):
    own_count, width = own_grad_ref.shape
    strip = REACH * SPAN
    top = place_ref[0] == 0
    bottom = place_ref[0] == place_ref[1] - 1
    parity = place_ref[2]
    odd_strip, even_strip = odd_ref[...], even_ref[1 - parity]
    west = jnp.where(parity == 0, odd_strip, even_strip)
    east = jnp.where(parity == 0, even_strip, odd_strip)
    gain = gain_ref[:, :width]
    weight = qkv_ref[...]
    group = head_group(width)

    def row_in(count):
        return lax.broadcasted_iota(jnp.int32, (count, 1), 0) & (SPAN - 1)

    def query_rows(count):
        row = row_in(count)
        own = row < 16
        below = (row >= 16) & (row < 16 + RADIUS) & jnp.logical_not(bottom)
        above = (row >= SPAN - RADIUS) & jnp.logical_not(top)
        return own | below | above

    def keys_of(cells, start):
        unit, reciprocal = unit_norm(cells)
        normed = (unit * gain).astype(BF16)
        keys, key_recip = head_norm(dot(normed, weight[:, width : 2 * width]), group)
        values = dot(normed, weight[:, 2 * width :])
        key_ref[start : start + cells.shape[0]] = keys.astype(BF16)
        value_ref[start : start + cells.shape[0]] = values.astype(BF16)
        return normed

    def queries_of(normed):
        return head_norm(dot(normed, weight[:, :width]), group)

    key_ref[strip : strip + own_count] = own_key_b_ref[...]
    value_ref[strip : strip + own_count] = own_value_b_ref[...]
    queries = own_query_ref[...]
    west_normed = keys_of(west[:strip], 0)
    east_normed = keys_of(east[:strip], strip + own_count)
    band = BAND * SPAN
    west_query = queries_of(west_normed[strip - band :])[0]
    east_query = queries_of(east_normed[:band])[0]

    own_grad = own_grad_ref[...]
    out_weight = out_ref[...]
    own_up = own_up_ref[...]
    west_up = dot(west[strip:], out_weight, 1, 1)
    east_up = dot(east[strip:], out_weight, 1, 1)
    empty = jnp.zeros((SPAN, width), F32)

    lane = lax.broadcasted_iota(jnp.int32, (1, width), 1) // HEAD_DIM
    zero = jnp.zeros((), BF16)

    def spread(cells, valid):
        cells = jnp.where(valid, cells, 0.0).astype(BF16)
        return jnp.concatenate([jnp.where(lane == head, cells, zero) for head in range(HEADS)], axis=0)

    rows_ok = query_rows(band)
    strip_col = lax.broadcasted_iota(jnp.int32, (band, 1), 0) // SPAN
    bands = (
        (spread(west_query, rows_ok & (strip_col > 0)), jnp.concatenate([empty, west_up], axis=0)),
        (spread(queries[:band], rows_ok), own_up[:band]),
        (spread(queries[band:], rows_ok), own_up[band:]),
        (spread(east_query, rows_ok & (strip_col < RADIUS)), jnp.concatenate([east_up, empty], axis=0)),
    )

    deep = (BAND + REACH) * SPAN
    key_at = lax.broadcasted_iota(jnp.int32, (deep, band), 0)
    query_at = lax.broadcasted_iota(jnp.int32, (deep, band), 1)
    col_gap = key_at // SPAN - query_at // SPAN
    row_gap = (key_at - query_at + RADIUS) & (SPAN - 1)
    inside = (col_gap >= 0) & (col_gap <= REACH) & (row_gap <= REACH)
    bias = jnp.where(inside, 0.0, LOWEST)
    bias = jnp.concatenate([bias] * HEADS, axis=1)
    lane_factors = [gain_ref[:, width + head : width + head + 1] * (1.0 / HEAD_DIM) for head in range(HEADS)]
    head_factor = jnp.zeros((1, width), F32)
    for head in range(HEADS):
        head_factor = jnp.where(lane == head, jnp.broadcast_to(lane_factors[head], (1, width)), head_factor)
    factor = jnp.concatenate(
        [
            jnp.broadcast_to(lane_factors[head], (1, band)) for head in range(HEADS)
        ],
        axis=1,
    ) * math.log2(math.e)

    def merge(stacked):
        half = width // 2
        low = lax.broadcasted_iota(jnp.int32, (1, half), 1) < HEAD_DIM
        parts = [stacked[head * band : (head + 1) * band] for head in range(HEADS)]
        return jnp.concatenate(
            [
                jnp.where(low, parts[0][:, :half], parts[1][:, :half]),
                jnp.where(low, parts[2][:, half:], parts[3][:, half:]),
            ],
            axis=1,
        )

    key_grad_ref[...] = jnp.zeros_like(key_grad_ref)
    value_grad_ref[...] = jnp.zeros_like(value_grad_ref)
    attended = []
    query_grads = []
    own_end = strip + own_count
    for index, (query_big, upstream) in enumerate(bands):
        up_big = spread(upstream, rows_ok)
        first = (2 + BAND * index - RADIUS) * SPAN
        last = first + deep
        lower, upper = max(first, 0), min(last, own_end + strip)
        key_band = key_ref[lower:upper]
        value_band = value_ref[lower:upper]
        scores = dot(key_band, query_big, 1, 1) * factor + bias[lower - first : upper - first]
        exponent = jnp.exp2(scores - jnp.max(scores, axis=0, keepdims=True))
        prob = exponent * (1.0 / jnp.sum(exponent, axis=0, keepdims=True))
        dots = dot(value_band, up_big, 1, 1)
        mean_dot = jnp.sum(prob * dots, axis=0, keepdims=True)
        weighted = (prob * (dots - mean_dot)).astype(BF16)
        prob = prob.astype(BF16)
        near, far = max(lower, strip), min(upper, own_end)
        key_grad_ref[near - strip : far - strip] += dot(weighted[near - lower : far - lower], query_big)
        value_grad_ref[near - strip : far - strip] += dot(prob[near - lower : far - lower], up_big)
        if index in (1, 2):
            attended.append(merge(dot(prob, value_band, 0, 0)))
            query_grads.append(merge(dot(weighted, key_band, 0, 0)))

    row = row_in(own_count)
    own_rows = row < 16
    key_rows = own_rows | (top & (row >= SPAN - RADIUS)) | (bottom & (row >= 16) & (row < 16 + RADIUS))
    query_grad = jnp.concatenate(query_grads, axis=0) * head_factor
    raw_query = head_back(query_grad, queries, own_query_recip_ref[...], group)
    raw_key = head_back(key_grad_ref[...] * head_factor, own_key_ref[...], own_key_recip_ref[...], group)
    projected_grad = jnp.concatenate(
        [
            jnp.where(own_rows, raw_query, 0.0),
            jnp.where(key_rows, raw_key, 0.0),
            jnp.where(key_rows, value_grad_ref[...], 0.0),
        ],
        axis=1,
    )
    projected_high = projected_grad.astype(BF16)
    projected_low = (projected_grad - projected_high.astype(F32)).astype(BF16)
    unit, normed = own_unit_ref[...], own_normed_ref[...]
    normed_grad = dot(projected_high, weight, 1, 1) + dot(projected_low, weight, 1, 1)
    gain_grad = jnp.sum(normed_grad * unit, axis=0, keepdims=True)
    normed_grad_ref[...] = normed_grad
    attended = jnp.where(own_rows, jnp.concatenate(attended, axis=0), 0.0).astype(BF16)
    weight_grad = dot(projected_high, normed, 0, 0)
    proj_grad = dot(own_grad, attended, 0, 0)
    for block in range(width // LANES):
        at = slice(block * LANES, (block + 1) * LANES)
        weight_grad_ref[block] = weight_grad[:, at]
        proj_grad_ref[block] = proj_grad[:, at]
    peers, rows = chunk_ref.shape[1:3]
    group = (rows - TAIL) // 8
    for index in range(2 * peers):
        peer, side = index // 2, index % 2
        line, lower = peer // lowers, peer % lowers
        half = (place_ref[0] + side) % 2
        column = line * group * lowers + lower
        for part in range(4):
            for block in range(width // LANES):
                if part < 3:
                    cells_ref, start, stride = weight_grad_ref, 6 * column + 3 * side + part, 6 * lowers
                else:
                    cells_ref, start, stride = proj_grad_ref, 2 * column + side, 2 * lowers
                at = (2 * part + block) * group
                cells = cells_ref.at[block][pl.ds(start, group, stride=stride), :]
                chunk_ref[half, peer, at : at + group] = cells.astype(BF16)
        lanes = gain_grad[:, 2 * column // LANES * LANES :][:, :LANES]
        chunk_ref[half, peer, rows - TAIL :] = high_low(lanes, TAIL, 2 * half)


def token_kernel(normed_grad_ref, unit_ref, scale_ref, own_grad_ref, gain_ref, token_ref):
    unit = unit_ref[...]
    scaled = normed_grad_ref[...] * gain_ref[:, : unit.shape[1]]
    token_part = scale_ref[:, :1] * (scaled - unit * jnp.mean(scaled * unit, axis=-1, keepdims=True))
    token_ref[...] = (own_grad_ref[...].astype(F32) + token_part).astype(BF16)


def middle_kernel(chunk_ref, part_ref, sum_ref):
    group = sum_ref.shape[0] // 8
    copies = part_ref.shape[0] // group
    total = sum(chunk_ref[peer].astype(F32) for peer in range(chunk_ref.shape[0]))
    sum_ref[...] = total[: 8 * group]
    gains = high_low(jnp.sum(total[8 * group :], axis=0, keepdims=True), TAIL - 8, 0).astype(F32)
    for column in range(group):
        rows = jnp.concatenate([sum_ref[pl.ds(column, 8, stride=group), :], gains], axis=0).astype(BF16)
        for copy in range(copies):
            part_ref[copies * column + copy] = rows


def final_kernel(scale, place_ref, parts_ref, qkv_ref, proj_ref, gain_ref):
    total = parts_ref[...] * scale
    lane = lax.broadcasted_iota(jnp.int32, (1, LANES), 1)
    gains = []
    for side in range(2):
        for part in range(4):
            at = side * TAIL + 2 * part
            row = jnp.concatenate([total[at : at + 1], total[at + 1 : at + 2]], axis=1)
            if part < 3:
                qkv_ref[3 * side + part : 3 * side + part + 1, :] = row
            else:
                proj_ref[side : side + 1, :] = row
        here = lane == 2 * place_ref[0] % LANES + side
        gains.append(jnp.sum(jnp.where(here, total[at + 2 : at + 3] + total[at + 3 : at + 4], 0.0), axis=1, keepdims=True))
    gain_ref[...] = jnp.concatenate(gains, axis=1)


def on_device(tokens, edge_tokens, output_grad, norm_gain, qkv_weight, out_weight, head_scale):
    row_count, col_count, width = tokens.shape
    row_devices = lax.axis_size(ROWS)
    col_devices = lax.axis_size(COLS)
    place = lax.axis_index(ROWS)
    grad_scale = (row_count * row_devices * col_count * col_devices) ** (-0.5)
    parity = lax.axis_index(COLS) & 1
    gains = jnp.concatenate([norm_gain, head_scale, jnp.zeros((LANES - HEADS,), F32)])[None, :]
    gains, tokens, output_grad = lax.optimization_barrier((gains, tokens, output_grad))
    strips = jnp.concatenate(
        [
            tokens[:REACH],
            tokens[row_count - REACH :],
            output_grad[:RADIUS],
            output_grad[row_count - RADIUS :],
        ],
        axis=0,
    )
    strips, edge_tokens, tokens, output_grad = lax.optimization_barrier(
        (lax.all_gather(strips, ROWS, axis=0), edge_tokens, tokens, output_grad)
    )
    strips = strips.transpose(0, 2, 1, 3)
    above = strips[jnp.maximum(place - 1, 0)]
    below = strips[jnp.minimum(place + 1, row_devices - 1)]
    own = tokens.transpose(1, 0, 2)
    grad = output_grad.transpose(1, 0, 2)
    edges = edge_tokens.transpose(2, 0, 1, 3)
    blank = jnp.zeros((col_count, RADIUS, width), BF16)
    upper = jnp.where(
        place == 0, jnp.concatenate([blank, edges[:, 0]], axis=1), above[:, REACH : 2 * REACH]
    )
    lower = jnp.where(
        place == row_devices - 1, jnp.concatenate([edges[:, 1], blank], axis=1), below[:, :REACH]
    )
    gap = jnp.zeros((col_count, SPAN - row_count - 2 * REACH, width), BF16)
    slab = jnp.concatenate([own, lower, gap, upper], axis=1)
    grad_gap = jnp.zeros((col_count, SPAN - row_count - 2 * RADIUS, width), BF16)
    grad_slab = jnp.concatenate(
        [
            grad,
            below[:, 2 * REACH : 2 * REACH + RADIUS],
            grad_gap,
            above[:, 2 * REACH + RADIUS :],
        ],
        axis=1,
    )
    facing_west = jnp.concatenate([slab[:REACH], grad_slab[:RADIUS]], axis=0)
    facing_east = jnp.concatenate([slab[col_count - REACH :], grad_slab[col_count - RADIUS :]], axis=0)
    first = [i for i in range(1, col_devices, 2)]
    pairs = [(i, (i + 1) % col_devices) for i in first]
    odd = lax.ppermute(
        jnp.where(parity == 0, facing_west, facing_east), COLS, pairs + [(b, a) for a, b in pairs]
    )
    even = lax.all_gather(
        jnp.where(parity == 0, facing_east, facing_west),
        COLS,
        axis=0,
        axis_index_groups=[[i, i + 1] for i in range(0, col_devices, 2)],
    )
    cells = col_count * SPAN
    lowers = lax.axis_size("v")
    peers = lax.axis_size("x") * lowers
    group = col_devices // peers
    whole = pl.BlockSpec(memory_space=pltpu.VMEM)
    scalars = pl.BlockSpec(memory_space=pltpu.SMEM)
    even, slab, grad_slab = lax.optimization_barrier((even, slab, grad_slab))
    wide = jax.ShapeDtypeStruct((cells, width), F32)
    narrow = jax.ShapeDtypeStruct((cells, width), BF16)
    own_parts = pl.pallas_call(
        own_kernel,
        out_shape=(
            wide,
            jax.ShapeDtypeStruct((cells, LANES), F32),
            narrow,
            wide,
            wide,
            narrow,
            narrow,
            wide,
            wide,
            wide,
        ),
        in_specs=[whole] * 5,
        out_specs=(whole,) * 10,
        compiler_params=pltpu.CompilerParams(vmem_limit_bytes=16 * 2**20),
    )(
        slab.reshape(cells, width),
        grad_slab.reshape(cells, width),
        gains,
        qkv_weight,
        out_weight,
    )
    unit, reciprocal, *own_parts = own_parts
    normed_grad, chunks = pl.pallas_call(
        functools.partial(block_kernel, lowers),
        out_shape=(
            jax.ShapeDtypeStruct((cells, width), F32),
            jax.ShapeDtypeStruct((2, peers, 8 * group + TAIL, LANES), BF16),
        ),
        in_specs=[scalars] + [whole] * 15,
        out_specs=(whole,) * 2,
        scratch_shapes=[
            pltpu.VMEM((cells + 2 * REACH * SPAN, width), BF16),
            pltpu.VMEM((cells + 2 * REACH * SPAN, width), BF16),
            pltpu.VMEM((cells, width), F32),
            pltpu.VMEM((cells, width), F32),
            pltpu.VMEM((width // LANES, 3 * width, LANES), F32),
            pltpu.VMEM((width // LANES, width, LANES), F32),
        ],
        compiler_params=pltpu.CompilerParams(vmem_limit_bytes=40 * 2**20),
    )(
        jnp.stack([place, row_devices, parity]).astype(jnp.int32),
        grad_slab.reshape(cells, width),
        odd.reshape(-1, width),
        even.reshape(2, -1, width),
        gains,
        qkv_weight,
        out_weight,
        unit,
        *own_parts,
    )
    token_grad = pl.pallas_call(
        token_kernel,
        out_shape=jax.ShapeDtypeStruct((cells, width), BF16),
        in_specs=[whole] * 5,
        out_specs=whole,
        compiler_params=pltpu.CompilerParams(vmem_limit_bytes=8 * 2**20),
        cost_estimate=pl.CostEstimate(flops=16 * cells * width, bytes_accessed=8 * cells * width, transcendentals=0),
    )(normed_grad, unit, reciprocal, grad_slab.reshape(cells, width), gains)
    token_grad = token_grad.reshape(col_count, SPAN, width)[:, :row_count].transpose(1, 0, 2)
    received = lax.all_gather(chunks[1].reshape(-1, LANES), "c", axis=0)[1 - lax.axis_index("c")]
    chunks = (chunks[0].astype(F32) + received.reshape(chunks.shape[1:]).astype(F32)).astype(BF16)
    chunks = lax.all_to_all(chunks, ("x", "v"), 0, 0)
    halves = lax.axis_size("h")
    part = pl.pallas_call(
        middle_kernel,
        out_shape=jax.ShapeDtypeStruct((halves * group, TAIL, LANES), BF16),
        in_specs=[whole],
        out_specs=whole,
        scratch_shapes=[pltpu.VMEM((8 * group, LANES), F32)],
        compiler_params=pltpu.CompilerParams(vmem_limit_bytes=8 * 2**20),
    )(chunks)
    part = jnp.sum(lax.all_to_all(part, ("l", "u", "h"), 0, 0).astype(F32), axis=0)
    qkv_grad, proj_grad, gain_grad = pl.pallas_call(
        functools.partial(final_kernel, grad_scale),
        out_shape=(
            jax.ShapeDtypeStruct((6, width), F32),
            jax.ShapeDtypeStruct((2, width), F32),
            jax.ShapeDtypeStruct((1, 2), F32),
        ),
        in_specs=[scalars, whole],
        out_specs=(whole,) * 3,
        compiler_params=pltpu.CompilerParams(vmem_limit_bytes=4 * 2**20),
    )(lax.axis_index(COLS)[None].astype(jnp.int32), lax.all_gather(part, "c", axis=0, tiled=True))
    return token_grad, qkv_grad.T, proj_grad.T, gain_grad.reshape(2)


def solution(mesh):
    parts = SPLIT + (2, 2)
    fine = jax.sharding.Mesh(mesh.devices.reshape(parts), COLS + ROWS)
    return jax.shard_map(
        on_device,
        mesh=fine,
        in_specs=(
            P(ROWS, COLS, None),
            P(None, None, COLS, None),
            P(ROWS, COLS, None),
            P(),
            P(),
            P(),
            P(),
        ),
        out_specs=(P(ROWS, COLS, None), P(None, COLS), P(None, COLS), P(COLS)),
        check_vma=False,
    )
```
